32 devices in a mesh: section: 4 (over y, x), dp: 8 (over z, core).
Axes of the slice: x: 2, y: 2, z: 4, core: 2. Of those that a mesh axis runs over, the one named last changes fastest.
Arguments:
- tokens: bfloat16 [2048, 4096], P('dp'), may hold values from -6 to 6
- cotangent: bfloat16 [2048, 4096], P('dp'), may hold values from -30 to 30
- lengths: int32 [32], P('dp'), may hold values from 1 to 64
- seq_user: int32 [32], P('dp'), may hold values from 0 to 15, as said below
- norm_gains: float32 [4, 4096], P('section'), may hold values from 0.5 to 1.5
- weights: float32 [4, 4096, 2, 256], P('section', 'dp'), may hold values from -1 to 1
- first_moment: float32 [4, 4096, 2, 256], P('section', 'dp'), may hold values from -6 to 6
- second_moment: float32 [4, 4096, 2, 256], P('section', 'dp'), may hold values from 0.25 to 4
Outputs:
- new_first: float32 [4, 4096, 2, 256], P('section', 'dp')
- new_second: float32 [4, 4096, 2, 256], P('section', 'dp')
- step_dir: float32 [4, 4096, 2, 256], P('section', 'dp')
- user_ratio: float32 [16], P('dp')
The draws below stay inside these ranges and needn't reach their ends.
Inputs may be any that keep to these rules, and one draw needn't show every extreme that they name: `seq_user`: the i-th block of 4 sequences carries only the user ids i * 2 to i * 2 + 1, each of them at least once.
All inputs are finite; a program needn't handle non-finite values.
Results may differ from the reference program's by a relative error of at most 0.0045.
Values may be sent and summed in bfloat16 or wider, within the bound.
A program may use at most 128 MiB of HBM per device.

```python
import math
import jax
import jax.numpy as jnp
from jax import lax

D = 4096
K = 256
SEQLEN = 64
SEQS_DEV = 4
TOK_DEV = 256
USERS_DEV = 2
SEQS = 32
TOKENS = 2048
USERS = 16
SECTIONS = 4
N_SECTION = 4
N_DP = 8


def draw_cotangent(key, part):
    key_one, key_two, key_three = jax.random.split(key, 3)
    base_values = jnp.clip(jax.random.normal(key_one, (TOKENS, D), jnp.float32), -5.0, 5.0)
    row_scale = jnp.exp(jax.random.uniform(key_two, (TOKENS, 1), jnp.float32, math.log(0.3), math.log(3.0)))
    col_scale = jnp.exp(jax.random.uniform(key_three, (1, D), jnp.float32, math.log(0.5), math.log(2.0)))
    return (base_values * row_scale * col_scale).astype(jnp.bfloat16)


def draw_lengths(key, part):
    drawn_lengths = jax.random.randint(key, (SEQS,), 1, SEQLEN + 1)
    return drawn_lengths.at[0].set(SEQLEN).astype(jnp.int32)


def draw_seq_user(key, part):
    devices = SEQS // SEQS_DEV
    device_keys = jax.random.split(key, devices)

    def one_device(device_key, device_no):
        key_one, key_two = jax.random.split(device_key)
        extra_users = jax.random.randint(key_one, (SEQS_DEV,), 0, USERS_DEV)
        slots = jnp.arange(SEQS_DEV)
        base_users = jnp.where(slots < USERS_DEV, slots, extra_users)
        shuffled = jax.random.permutation(key_two, base_users)
        return (shuffled + device_no * USERS_DEV).astype(jnp.int32)
    return jax.vmap(one_device)(device_keys, jnp.arange(devices)).reshape(SEQS).astype(jnp.int32)


def draw_weights(key, part):
    normal_raw = jnp.clip(jax.random.normal(key, (SECTIONS, D, 2, K), jnp.float32), -6.0, 6.0)
    column_scale = jnp.array([D ** (-0.5), K ** (-0.5)], jnp.float32)
    return normal_raw * column_scale[None, None, :, None]


def block_scale(rng, shape, cuts, low, high):
    def one(axis_at, shards_of):
        heights = jax.random.uniform(jax.random.fold_in(jax.random.fold_in(rng, 6), axis_at), (shards_of,), jnp.float32, low / len(cuts), high / len(cuts))
        return jnp.repeat(jnp.exp(heights), shape[axis_at] // shards_of).reshape((-1,) + (1,) * (len(shape) - axis_at - 1))

    loudness = one(*cuts[0])
    for cut in cuts[1:]:
        loudness = loudness * one(*cut)
    return loudness


def centred(rng, dims, scale, bound, cuts=(), dtype=jnp.bfloat16):
    result = jax.random.normal(rng, dims, jnp.float32) * scale
    if len(cuts) > 0:
        result = block_scale(rng, dims, cuts, -0.22, 0.18) * result
    return jnp.clip(result, min=-bound, max=bound).astype(dtype)


def setup_inputs(seed: int = 0) -> dict:
    streams_of = jax.random.split(jax.random.key(seed), 9)
    return {
        "tokens": centred(streams_of[0], (TOKENS, D), 1.0, 6.0, ((0, 8),)),
        "cotangent": draw_cotangent(jax.random.fold_in(streams_of[8], 71), 0),
        "lengths": draw_lengths(jax.random.fold_in(streams_of[8], 71), 0),
        "seq_user": draw_seq_user(jax.random.fold_in(streams_of[8], 71), 0),
        "norm_gains": jnp.clip(1.0 + 0.1 * jax.random.normal(streams_of[4], (SECTIONS, D), jnp.float32), 0.5, 1.5),
        "weights": draw_weights(jax.random.fold_in(streams_of[8], 71), 0),
        "first_moment": centred(streams_of[6], (SECTIONS, D, 2, K), 1.0, 6.0, ((0, 4), (1, 8)), jnp.float32),
        "second_moment": jnp.clip(jnp.exp(math.log(4.0) - 2.7725887 * jax.random.uniform(streams_of[7], (SECTIONS, D, 2, K), jnp.float32) ** block_scale(streams_of[7], (SECTIONS, D, 2, K), ((0, 4), (1, 8)), -0.2, 0.2)), 0.25, 4.0),
    }


CLIP_BOUND = 70000.0
LOSS_SCALE = 1024.0
BETA_ONE = 0.9
BETA_TWO = 0.999
FIRST_FIX = 1.0 - 0.9 ** 50
SECOND_FIX = 1.0 - 0.999 ** 50
ADAM_EPS = 1e-08
NORM_EPS = 1e-05

def section_forward(hidden, section_gain, down_cast, up_cast):
    widened = hidden.astype(jnp.float32)
    inverse = lax.rsqrt(lax.optimization_barrier(jnp.mean(widened * widened, axis=-1, keepdims=True)) + NORM_EPS)
    normed = (widened * inverse * section_gain).astype(jnp.bfloat16)
    inner_act = jnp.dot(normed, down_cast, preferred_element_type=jnp.float32)
    active = jax.nn.silu(inner_act).astype(jnp.bfloat16)
    branch = lax.dot_general(active, up_cast, (((1,), (1,)), ((), ())), preferred_element_type=jnp.float32)
    return ((widened + branch).astype(jnp.bfloat16), (widened, inverse, normed, inner_act, active))

def section_backward(grad_out, section_gain, down_cast, up_cast, kept_acts):
    widened, inverse, normed, inner_act, active = kept_acts
    grad_active = jnp.dot(grad_out, up_cast, preferred_element_type=jnp.float32)
    sigmoid_val = jax.nn.sigmoid(inner_act)
    grad_inner = (grad_active * sigmoid_val * (1.0 + inner_act * (1.0 - sigmoid_val))).astype(jnp.bfloat16)
    grad_normed = lax.dot_general(grad_inner, down_cast, (((1,), (1,)), ((), ())), preferred_element_type=jnp.float32)
    scaled = grad_normed * section_gain
    projected = lax.optimization_barrier(jnp.mean(scaled * widened, axis=-1, keepdims=True))
    grad_in = grad_out.astype(jnp.float32) + inverse * scaled - widened * inverse * inverse * inverse * projected
    return (grad_in.astype(jnp.bfloat16), grad_inner)

def gram_of(values):
    return lax.dot_general(values, values, (((1,), (1,)), ((), ())), preferred_element_type=jnp.float32)

def user_squares(normed, grad_inner, active, grad_out, owners):
    joint = gram_of(normed) * gram_of(grad_inner) + gram_of(active) * gram_of(grad_out)
    spread = jnp.dot(joint, owners, precision=lax.Precision.HIGHEST)
    return lax.optimization_barrier(jnp.sum(spread * owners, axis=0))

def reference(tokens, cotangent, lengths, seq_user, norm_gains, weights, first_moment, second_moment):
    low_weights = weights.astype(jnp.bfloat16)
    hidden = tokens
    saved_all = []
    for section_no in range(N_SECTION):
        hidden, kept_acts = section_forward(hidden, norm_gains[section_no], low_weights[section_no, :, 0, :], low_weights[section_no, :, 1, :])
        saved_all.append(kept_acts)
    positions = jnp.arange(TOKENS) % SEQLEN
    usable = positions < jnp.repeat(lengths, SEQLEN)
    token_user = jnp.repeat(seq_user, SEQLEN)
    owners = ((token_user[:, None] == jnp.arange(USERS)[None, :]) & usable[:, None]).astype(jnp.float32)
    grad_out = cotangent * usable[:, None].astype(jnp.bfloat16)
    records = [None] * N_SECTION
    for section_no in reversed(range(N_SECTION)):
        grad_in, grad_inner = section_backward(grad_out, norm_gains[section_no], low_weights[section_no, :, 0, :], low_weights[section_no, :, 1, :], saved_all[section_no])
        records[section_no] = (grad_out, grad_inner)
        grad_out = grad_in
    squares = jnp.zeros((USERS,), jnp.float32)
    owner_blocks = owners.reshape(N_DP, TOK_DEV, USERS)
    for section_no in range(N_SECTION):
        members = (saved_all[section_no][2].reshape(N_DP, TOK_DEV, D), records[section_no][1].reshape(N_DP, TOK_DEV, K), saved_all[section_no][4].reshape(N_DP, TOK_DEV, K), records[section_no][0].reshape(N_DP, TOK_DEV, D), owner_blocks)
        per_device = lax.map(lambda group_in: user_squares(*group_in), members)
        squares = squares + lax.optimization_barrier(jnp.sum(per_device, axis=0))
    user_norm = jnp.sqrt(squares)
    user_ratio = user_norm / CLIP_BOUND
    factors = LOSS_SCALE / jnp.maximum(user_norm, CLIP_BOUND)
    token_factor = jnp.dot(owners, factors, precision=lax.Precision.HIGHEST)
    grads_all = []
    for section_no in range(N_SECTION):
        grad_out, grad_inner = records[section_no]
        weighted_inner = (grad_inner.astype(jnp.float32) * token_factor[:, None]).astype(jnp.bfloat16)
        weighted_out = (grad_out.astype(jnp.float32) * token_factor[:, None]).astype(jnp.bfloat16)
        down_term = lax.dot_general(saved_all[section_no][2], weighted_inner, (((0,), (0,)), ((), ())), preferred_element_type=jnp.float32)
        up_term = lax.dot_general(weighted_out, saved_all[section_no][4], (((0,), (0,)), ((), ())), preferred_element_type=jnp.float32)
        grads_all.append(jnp.stack([down_term, up_term], axis=1))
    gradient = jnp.stack(grads_all, axis=0)
    new_first = BETA_ONE * first_moment + (1.0 - BETA_ONE) * gradient
    new_second = BETA_TWO * second_moment + (1.0 - BETA_TWO) * gradient * gradient
    step_dir = new_first / FIRST_FIX / (jnp.sqrt(new_second / SECOND_FIX) + ADAM_EPS)
    return (new_first, new_second, step_dir, user_ratio)
```

```python
import jax
import jax.numpy as jnp
from jax import lax
from jax.sharding import PartitionSpec as P

SEQLEN = 64
USERS_DEV = 2


CLIP_BOUND = 70000.0
LOSS_SCALE = 1024.0
BETA_ONE = 0.9
BETA_TWO = 0.999
FIRST_FIX = 1.0 - 0.9**50
SECOND_FIX = 1.0 - 0.999**50
ADAM_EPS = 1e-08
NORM_EPS = 1e-05


def dot_nt(left, right):
    return lax.dot_general(
        left, right, (((1,), (1,)), ((), ())), preferred_element_type=jnp.float32
    )


def dot_tn(left, right):
    return lax.dot_general(
        left, right, (((0,), (0,)), ((), ())), preferred_element_type=jnp.float32
    )


def on_device(
    tokens, cotangent, lengths, seq_user, norm_gains, weights, first_moment, second_moment
):
    sections = lax.axis_size("section")
    quarter = lax.axis_index("section")
    shards = lax.axis_size("dp")
    tok_rows, model_width = tokens.shape
    own_rows, _, width = weights.shape[1:]
    part = own_rows // sections
    held = shards * part

    def own_features(values):
        split = values.reshape(tok_rows, shards, sections, part)
        return lax.dynamic_index_in_dim(split, quarter, 2, keepdims=False).reshape(tok_rows, held)

    low = weights[0].astype(jnp.bfloat16).reshape(sections, part, 2, width)
    low = lax.all_to_all(low.transpose(0, 2, 1, 3), "section", 0, 0, tiled=True)
    low = lax.all_gather(low, "dp", axis=2, tiled=True)
    gains = norm_gains[0].reshape(shards, sections, part).transpose(1, 0, 2)
    gains = lax.all_to_all(gains.reshape(sections, held), "section", 0, 0, tiled=True)

    positions = jnp.arange(tok_rows) % SEQLEN
    usable = positions < jnp.repeat(lengths, SEQLEN)
    local_user = seq_user - lax.axis_index("dp") * USERS_DEV
    token_user = jnp.repeat(local_user, SEQLEN)
    owners = ((token_user[:, None] == jnp.arange(USERS_DEV)[None, :]) & usable[:, None]).astype(
        jnp.float32
    )

    hidden = own_features(tokens)
    kept = []
    for s in range(sections):
        down, up = low[s, 0], low[s, 1]
        widened = hidden.astype(jnp.float32)
        scaled = (widened * gains[s]).astype(jnp.bfloat16)
        product = jnp.dot(scaled, down, preferred_element_type=jnp.float32)
        total, product = lax.psum(
            (jnp.sum(widened * widened, axis=-1, keepdims=True), product), "section"
        )
        inverse = lax.rsqrt(total / model_width + NORM_EPS)
        inner = product * inverse
        active = jax.nn.silu(inner).astype(jnp.bfloat16)
        kept.append((widened, scaled, inverse, inner, active))
        hidden = (widened + dot_nt(active, up)).astype(jnp.bfloat16)

    grad_out = own_features(cotangent) * usable[:, None].astype(jnp.bfloat16)
    records = [None] * sections
    joint = jnp.zeros((tok_rows, tok_rows), jnp.float32)
    for s in reversed(range(sections)):
        down, up = low[s, 0], low[s, 1]
        widened, scaled, inverse, inner, active = kept[s]
        grad_active = lax.psum(
            jnp.dot(grad_out, up, preferred_element_type=jnp.float32), "section"
        )
        sigmoid_val = jax.nn.sigmoid(inner)
        grad_inner = grad_active * sigmoid_val * (1.0 + inner * (1.0 - sigmoid_val))
        grad_scaled = (grad_inner * inverse).astype(jnp.bfloat16)
        pull = jnp.sum(grad_inner * inner, axis=-1, keepdims=True) * (
            inverse * inverse / model_width
        )
        records[s] = (scaled, grad_scaled, grad_out, active)
        joint = joint + dot_nt(scaled, scaled) * dot_nt(grad_scaled, grad_scaled)
        joint = joint + dot_nt(active, active) * dot_nt(grad_out, grad_out)
        if s > 0:
            grad_out = (
                grad_out.astype(jnp.float32)
                + gains[s] * dot_nt(grad_scaled, down)
                - widened * pull
            ).astype(jnp.bfloat16)

    spread = jnp.dot(joint, owners, precision=lax.Precision.HIGHEST)
    squares = lax.psum(jnp.sum(spread * owners, axis=0), "section")
    user_norm = jnp.sqrt(squares)
    factors = LOSS_SCALE / jnp.maximum(user_norm, CLIP_BOUND)
    token_factor = jnp.dot(owners, factors, precision=lax.Precision.HIGHEST)[:, None]
    terms = []
    for scaled, grad_scaled, grad_out, active in records:
        weighted_inner = (grad_scaled.astype(jnp.float32) * token_factor).astype(jnp.bfloat16)
        weighted_out = (grad_out.astype(jnp.float32) * token_factor).astype(jnp.bfloat16)
        terms.append(
            jnp.stack([dot_tn(scaled, weighted_inner), dot_tn(weighted_out, active)], axis=0)
        )
    gradient = jnp.stack(terms, axis=0).astype(jnp.bfloat16)
    gradient = lax.psum_scatter(gradient, "dp", scatter_dimension=2, tiled=True)
    gradient = lax.all_to_all(gradient, "section", 0, 0, tiled=True)
    gradient = gradient.transpose(0, 2, 1, 3).reshape(own_rows, 2, width).astype(jnp.float32)
    moment_one = BETA_ONE * first_moment[0] + (1.0 - BETA_ONE) * gradient
    moment_two = BETA_TWO * second_moment[0] + (1.0 - BETA_TWO) * gradient * gradient
    direction = moment_one / FIRST_FIX / (jnp.sqrt(moment_two / SECOND_FIX) + ADAM_EPS)
    return (moment_one[None], moment_two[None], direction[None], user_norm / CLIP_BOUND)


def solution(mesh):
    return jax.shard_map(
        on_device,
        mesh=mesh,
        in_specs=(
            P("dp", None),
            P("dp", None),
            P("dp"),
            P("dp"),
            P("section", None),
            P("section", "dp", None, None),
            P("section", "dp", None, None),
            P("section", "dp", None, None),
        ),
        out_specs=(
            P("section", "dp", None, None),
            P("section", "dp", None, None),
            P("section", "dp", None, None),
            P("dp"),
        ),
        check_vma=False,
    )
```

```python
import functools

import jax
import jax.numpy as jnp
from jax import lax
from jax.experimental import pallas as pl
from jax.experimental.pallas import tpu as pltpu
from jax.sharding import PartitionSpec as P

SEQLEN = 64
USERS_DEV = 2


CLIP_BOUND = 70000.0
LOSS_SCALE = 1024.0
BETA_ONE = 0.9
BETA_TWO = 0.999
FIRST_FIX = 1.0 - 0.9**50
SECOND_FIX = 1.0 - 0.999**50
ADAM_EPS = 1e-08
NORM_EPS = 1e-05
LANES = 128


def dot_nt(left, right):
    return lax.dot_general(
        left, right, (((1,), (1,)), ((), ())), preferred_element_type=jnp.float32
    )


def dot_tn(left, right):
    return lax.dot_general(
        left, right, (((0,), (0,)), ((), ())), preferred_element_type=jnp.float32
    )


def split_lanes(column, rows):
    wide = jnp.broadcast_to(column, (rows, LANES))
    high = wide.astype(jnp.bfloat16).astype(jnp.float32)
    lane = lax.broadcasted_iota(jnp.int32, (rows, LANES), 1)
    return jnp.where(lane < LANES // 2, high, wide - high).astype(jnp.bfloat16)


def joined_lanes(block, start):
    high = block[:, start : start + 1].astype(jnp.float32)
    return high + block[:, start + LANES // 2 : start + LANES // 2 + 1].astype(jnp.float32)


def chain_kernel(
    sections,
    model_width,
    tokens_ref,
    cotangent_ref,
    gains_ref,
    owners_ref,
    owners_row_ref,
    low_ref,
    gradient_ref,
    norm_ref,
    hidden,
    scaled,
    grad_out,
    active,
    grad_scaled,
    inner,
    inverse,
    own_part,
    outgoing,
    landed,
    joint,
    squares,
    send_sem,
    recv_sem,
):
    me = lax.axis_index("section")
    tok_rows, held = tokens_ref.shape
    width = active.shape[2]
    block = tok_rows // sections
    own = pl.ds(pl.multiple_of(me * block, block), block)
    peers = [lax.rem(me + d, sections) for d in range(1, sections)]

    barrier = pltpu.get_barrier_semaphore()
    for peer in peers:
        pl.semaphore_signal(
            barrier, inc=1, device_id={"section": peer}, device_id_type=pl.DeviceIdType.MESH
        )
    pl.semaphore_wait(barrier, sections - 1)

    def copies(make, slot):
        return [
            pltpu.make_async_remote_copy(
                src_ref=source,
                dst_ref=target,
                send_sem=send_sem.at[slot, d],
                recv_sem=recv_sem.at[slot, d],
                device_id={"section": peers[d]},
                device_id_type=pl.DeviceIdType.MESH,
            )
            for d in range(sections - 1)
            for source, target in [make(d)]
        ]

    def to_owners(step):
        def make(d):
            rows = pl.ds(pl.multiple_of(peers[d] * block, block), block)
            return outgoing.at[step, rows], landed.at[step, d]

        return copies(make, 2 * step)

    def to_all(ref, s, step):
        def make(d):
            return ref.at[s, own], ref.at[s, own]

        return copies(make, 2 * step + 1)

    def start(sent):
        for copy in sent:
            copy.start()

    def arrived(sent):
        for copy in sent:
            copy.wait_recv()

    hidden[0] = tokens_ref[...]
    joint[...] = jnp.zeros_like(joint)

    def forward(s, carry):
        widened = hidden[s].astype(jnp.float32)
        now = (widened * gains_ref[s]).astype(jnp.bfloat16)
        scaled[s] = now
        product = jnp.dot(now, low_ref[s, 0], preferred_element_type=jnp.float32)
        square = jnp.sum(widened * widened, axis=-1, keepdims=True)
        own_part[:, :width] = product
        own_part[:, width:] = jnp.broadcast_to(square, (tok_rows, LANES))
        outgoing[s, :, :width] = product.astype(jnp.bfloat16)
        outgoing[s, :, width:] = split_lanes(square, tok_rows)
        sent = to_owners(s)
        start(sent)
        arrived(sent)
        total = own_part[own, :width]
        mean = own_part[own, width : width + 1]
        for d in range(sections - 1):
            piece = landed[s, d]
            total = total + piece[:, :width].astype(jnp.float32)
            mean = mean + joined_lanes(piece, width)
        scale = lax.rsqrt(mean / model_width + NORM_EPS)
        value = total * scale
        inner[s] = value
        inverse[s] = jnp.broadcast_to(scale, (block, LANES))
        active[s, own] = (value / (1.0 + jnp.exp(-value))).astype(jnp.bfloat16)
        sent = to_all(active, s, s)
        start(sent)
        arrived(sent)

        @pl.when(s < sections - 1)
        def _():
            branch = dot_nt(active[s], low_ref[s, 1])
            hidden[s + 1] = (hidden[s].astype(jnp.float32) + branch).astype(jnp.bfloat16)

        return carry

    lax.fori_loop(0, sections, forward, 0)
    grad_out[sections - 1] = cotangent_ref[...]

    def backward(back, carry):
        s = sections - 1 - back
        step = sections + back
        product = jnp.dot(grad_out[s], low_ref[s, 1], preferred_element_type=jnp.float32)
        own_part[:, :width] = product
        outgoing[step, :, :width] = product.astype(jnp.bfloat16)
        sent = to_owners(step)
        start(sent)
        joint[...] += dot_nt(active[s], active[s]) * dot_nt(grad_out[s], grad_out[s])
        arrived(sent)
        total = own_part[own, :width]
        for d in range(sections - 1):
            total = total + landed[step, d, :, :width].astype(jnp.float32)
        value = inner[s]
        scale = inverse[s][:, :1]
        sigmoid_val = 1.0 / (1.0 + jnp.exp(-value))
        grad_inner = total * sigmoid_val * (1.0 + value * (1.0 - sigmoid_val))
        pull = jnp.sum(grad_inner * value, axis=-1, keepdims=True) * (
            scale * scale / model_width
        )
        grad_scaled[s, own, :width] = (grad_inner * scale).astype(jnp.bfloat16)
        grad_scaled[s, own, width:] = split_lanes(pull, block)
        sent = to_all(grad_scaled, s, step)
        start(sent)
        gram = dot_nt(scaled[s], scaled[s])
        arrived(sent)
        whole = grad_scaled[s]
        low_grad = whole[:, :width]

        @pl.when(s > 0)
        def _():
            grad_out[s - 1] = (
                grad_out[s].astype(jnp.float32)
                + gains_ref[s] * dot_nt(low_grad, low_ref[s, 0])
                - hidden[s].astype(jnp.float32) * joined_lanes(whole, width)
            ).astype(jnp.bfloat16)

        joint[...] += gram * dot_nt(low_grad, low_grad)
        return carry

    lax.fori_loop(0, sections, backward, 0)

    row_of = lax.broadcasted_iota(jnp.int32, (8, LANES), 0)
    sums = jnp.zeros((8, LANES), jnp.float32)
    for user in range(USERS_DEV):
        spread = joint[...] * owners_row_ref[user : user + 1, :]
        held_sum = jnp.sum(spread, axis=-1, keepdims=True) * owners_ref[:, user : user + 1]
        whole_sum = jnp.sum(held_sum, axis=0, keepdims=True)
        sums = jnp.where(row_of == user, whole_sum, sums)
    squares[me] = sums
    sent = copies(lambda d: (squares.at[me], squares.at[me]), 4 * sections)
    start(sent)
    arrived(sent)
    total = squares[0]
    for s in range(1, sections):
        total = total + squares[s]
    user_norm = jnp.sqrt(total)
    norm_ref[...] = user_norm
    factors = LOSS_SCALE / jnp.maximum(user_norm, CLIP_BOUND)
    token_factor = owners_ref[:, :1] * factors[:1, :1]
    for user in range(1, USERS_DEV):
        token_factor = token_factor + owners_ref[:, user : user + 1] * factors[user : user + 1, :1]

    def products(s, carry):
        weighted_inner = (grad_scaled[s, :, :width].astype(jnp.float32) * token_factor).astype(
            jnp.bfloat16
        )
        weighted_out = (grad_out[s].astype(jnp.float32) * token_factor).astype(jnp.bfloat16)
        gradient_ref[s, 0] = dot_tn(scaled[s], weighted_inner).astype(jnp.bfloat16)
        gradient_ref[s, 1] = dot_tn(weighted_out, active[s]).astype(jnp.bfloat16)
        return carry

    lax.fori_loop(0, sections, products, 0)

    def drain(step, carry):
        for copy in to_owners(step) + to_all(active, 0, step):
            copy.wait_send()
        return carry

    def drain_back(step, carry):
        for copy in to_owners(step) + to_all(grad_scaled, 0, step):
            copy.wait_send()
        return carry

    lax.fori_loop(0, sections, drain, 0)
    lax.fori_loop(sections, 2 * sections, drain_back, 0)
    for copy in sent:
        copy.wait_send()


def chain(tokens, cotangent, gains, owners, low, model_width):
    sections, _, held, width = low.shape
    tok_rows = tokens.shape[0]
    block = tok_rows // sections
    vmem = pl.BlockSpec(memory_space=pltpu.VMEM)
    owners_row = jnp.pad(owners.T, ((0, 8 - USERS_DEV), (0, 0)))
    owners = jnp.pad(owners, ((0, 0), (0, LANES - USERS_DEV)))
    steps = 2 * sections
    copies = (2 * steps + 1, sections - 1)
    bf16, f32 = jnp.bfloat16, jnp.float32
    return pl.pallas_call(
        functools.partial(chain_kernel, sections, model_width),
        out_shape=(
            jax.ShapeDtypeStruct(low.shape, bf16),
            jax.ShapeDtypeStruct((8, LANES), f32),
        ),
        in_specs=[vmem] * 6,
        out_specs=(vmem, vmem),
        scratch_shapes=[
            pltpu.VMEM((sections, tok_rows, held), bf16),
            pltpu.VMEM((sections, tok_rows, held), bf16),
            pltpu.VMEM((sections, tok_rows, held), bf16),
            pltpu.VMEM((sections, tok_rows, width), bf16),
            pltpu.VMEM((sections, tok_rows, width + LANES), bf16),
            pltpu.VMEM((sections, block, width), f32),
            pltpu.VMEM((sections, block, LANES), f32),
            pltpu.VMEM((tok_rows, width + LANES), f32),
            pltpu.VMEM((steps, tok_rows, width + LANES), bf16),
            pltpu.VMEM((steps, sections - 1, block, width + LANES), bf16),
            pltpu.VMEM((tok_rows, tok_rows), f32),
            pltpu.VMEM((sections, 8, LANES), f32),
            pltpu.SemaphoreType.DMA(copies),
            pltpu.SemaphoreType.DMA(copies),
        ],
        compiler_params=pltpu.CompilerParams(
            collective_id=0, has_side_effects=True, vmem_limit_bytes=48 * 1024 * 1024
        ),
    )(tokens, cotangent, gains[:, None, :], owners, owners_row, low)


def on_device(
    tokens, cotangent, lengths, seq_user, norm_gains, weights, first_moment, second_moment
):
    sections = lax.axis_size("section")
    quarter = lax.axis_index("section")
    shards = lax.axis_size("dp")
    tok_rows, model_width = tokens.shape
    own_rows, _, width = weights.shape[1:]
    part = own_rows // sections
    held = shards * part

    def own_features(values):
        split = values.reshape(tok_rows, shards, sections, part)
        return lax.dynamic_index_in_dim(split, quarter, 2, keepdims=False).reshape(tok_rows, held)

    low = weights[0].astype(jnp.bfloat16).reshape(sections, part, 2, width)
    low = lax.all_to_all(low.transpose(0, 2, 1, 3), "section", 0, 0, tiled=True)
    low = lax.all_gather(low, "dp", axis=2, tiled=True)
    gains = norm_gains[0].reshape(shards, sections, part).transpose(1, 0, 2)
    gains = lax.all_to_all(gains.reshape(sections, held), "section", 0, 0, tiled=True)

    positions = jnp.arange(tok_rows) % SEQLEN
    usable = positions < jnp.repeat(lengths, SEQLEN)
    local_user = seq_user - lax.axis_index("dp") * USERS_DEV
    token_user = jnp.repeat(local_user, SEQLEN)
    owners = ((token_user[:, None] == jnp.arange(USERS_DEV)[None, :]) & usable[:, None]).astype(
        jnp.float32
    )

    seeds = own_features(cotangent) * usable[:, None].astype(jnp.bfloat16)
    gradient, norms = chain(own_features(tokens), seeds, gains, owners, low, model_width)
    user_norm = norms[:USERS_DEV, 0]
    gradient = lax.psum_scatter(gradient, "dp", scatter_dimension=2, tiled=True)
    gradient = lax.all_to_all(gradient, "section", 0, 0, tiled=True)
    gradient = gradient.transpose(0, 2, 1, 3).reshape(own_rows, 2, width).astype(jnp.float32)
    moment_one = BETA_ONE * first_moment[0] + (1.0 - BETA_ONE) * gradient
    moment_two = BETA_TWO * second_moment[0] + (1.0 - BETA_TWO) * gradient * gradient
    direction = moment_one / FIRST_FIX / (jnp.sqrt(moment_two / SECOND_FIX) + ADAM_EPS)
    return (moment_one[None], moment_two[None], direction[None], user_norm / CLIP_BOUND)


def solution(mesh):
    return jax.shard_map(
        on_device,
        mesh=mesh,
        in_specs=(
            P("dp", None),
            P("dp", None),
            P("dp"),
            P("dp"),
            P("section", None),
            P("section", "dp", None, None),
            P("section", "dp", None, None),
            P("section", "dp", None, None),
        ),
        out_specs=(
            P("section", "dp", None, None),
            P("section", "dp", None, None),
            P("section", "dp", None, None),
            P("dp"),
        ),
        check_vma=False,
    )
```

```python
import functools

import jax
import jax.numpy as jnp
from jax import lax
from jax.experimental import pallas as pl
from jax.experimental.pallas import tpu as pltpu
from jax.sharding import PartitionSpec as P

SEQLEN = 64
USERS_DEV = 2


CLIP_BOUND = 70000.0
LOSS_SCALE = 1024.0
BETA_ONE = 0.9
BETA_TWO = 0.999
FIRST_FIX = 1.0 - 0.9**50
SECOND_FIX = 1.0 - 0.999**50
ADAM_EPS = 1e-08
NORM_EPS = 1e-05
LANES = 128


def dot_nt(left, right):
    return lax.dot_general(
        left, right, (((1,), (1,)), ((), ())), preferred_element_type=jnp.float32
    )


def dot_tn(left, right):
    return lax.dot_general(
        left, right, (((0,), (0,)), ((), ())), preferred_element_type=jnp.float32
    )


def split_lanes(column, rows):
    wide = jnp.broadcast_to(column, (rows, LANES))
    high = wide.astype(jnp.bfloat16).astype(jnp.float32)
    lane = lax.broadcasted_iota(jnp.int32, (rows, LANES), 1)
    return jnp.where(lane < LANES // 2, high, wide - high).astype(jnp.bfloat16)


def joined_lanes(block, start):
    high = block[:, start : start + 1].astype(jnp.float32)
    return high + block[:, start + LANES // 2 : start + LANES // 2 + 1].astype(jnp.float32)


def chain_kernel(
    sections,
    model_width,
    load_width,
    tokens_ref,
    cotangent_ref,
    own_gains_ref,
    owners_ref,
    owners_row_ref,
    rows_ref,
    gradient_ref,
    norm_ref,
    low,
    gains,
    hidden,
    scaled,
    grad_out,
    active,
    grad_scaled,
    inner,
    inverse,
    own_part,
    outgoing,
    landed,
    joint,
    squares,
    terms,
    sibling_terms,
    chip_sums,
    chip_landed,
    final_out,
    final_landed,
    send_sem,
    recv_sem,
    load_sem,
    rows_send,
    rows_recv,
    gains_send,
    gains_recv,
    along_send,
    along_recv,
    sibling_send,
    sibling_recv,
    pair_send,
    pair_recv,
    chip_send,
    chip_recv,
    final_send,
    final_recv,
):
    me = lax.axis_index("section")
    place = lax.axis_index("dp")
    chips = lax.axis_size("dp") // 2
    chip, core = place // 2, lax.rem(place, 2)
    sibling = chip * 2 + 1 - core
    _, tok_rows, held = hidden.shape
    width = active.shape[2]
    part = rows_ref.shape[2]
    block = tok_rows // sections
    own = pl.ds(pl.multiple_of(me * block, block), block)
    peers = [lax.rem(me + d, sections) for d in range(1, sections)]

    barrier = pltpu.get_barrier_semaphore()
    for peer in peers:
        pl.semaphore_signal(
            barrier, inc=1, device_id={"section": peer}, device_id_type=pl.DeviceIdType.MESH
        )
    ahead = [lax.rem(chip + d, chips) for d in range(1, chips)]
    behind = [lax.rem(chip + chips - d, chips) for d in range(1, chips)]
    for other in [sibling] + [a * 2 + core for a in ahead]:
        pl.semaphore_signal(
            barrier, inc=1, device_id={"dp": other}, device_id_type=pl.DeviceIdType.MESH
        )
    pl.semaphore_wait(barrier, sections - 1 + chips)

    def remote(source, target, sent, received, axis, index):
        return pltpu.make_async_remote_copy(
            src_ref=source,
            dst_ref=target,
            send_sem=sent,
            recv_sem=received,
            device_id={axis: index},
            device_id_type=pl.DeviceIdType.MESH,
        )

    def shard(s, at_chip, at_core):
        row = pl.multiple_of((at_chip * 2 + at_core) * part, part)
        return low.at[s, :, pl.ds(row, part)]

    pieces = held // load_width
    loads = []
    for which, (source, target) in enumerate(
        ((tokens_ref, hidden.at[0]), (cotangent_ref, grad_out.at[sections - 1]))
    ):
        for piece in range(pieces):
            first = (piece * sections + me) * load_width if pieces > 1 else 0
            loads.append(
                pltpu.make_async_copy(
                    source.at[:, pl.ds(pl.multiple_of(first, load_width), load_width)],
                    target.at[:, pl.ds(piece * load_width, load_width)],
                    load_sem.at[which, piece],
                )
            )

    def rows_copy(target, slot, source):
        return remote(
            rows_ref.at[target], shard(me, chip, core), rows_send.at[slot], rows_recv.at[source],
            "section", target,
        )

    def gains_copy(target, slot, source):
        return remote(
            own_gains_ref.at[target], gains.at[me], gains_send.at[slot], gains_recv.at[source],
            "section", target,
        )

    def along_copy(s, d):
        return remote(
            shard(s, chip, core), shard(s, chip, core), along_send.at[s, d], along_recv.at[s, d],
            "dp", ahead[d] * 2 + core,
        )

    def sibling_copy(s, slot, at_chip):
        return remote(
            shard(s, at_chip, core), shard(s, at_chip, core),
            sibling_send.at[s, slot], sibling_recv.at[s, slot], "dp", sibling,
        )

    for d in range(sections - 1):
        rows_copy(peers[d], d, me).start()
        gains_copy(peers[d], d, me).start()
    for load in loads:
        load.start()
    low[me, :, pl.ds(pl.multiple_of(place * part, part), part)] = rows_ref[me]
    gains[me] = own_gains_ref[me]

    def spread_rows(s, carry):
        @pl.when(s != me)
        def _():
            rows_copy(peers[0], 0, s).wait_recv()
            gains_copy(peers[0], 0, s).wait_recv()

        sibling_copy(s, 0, chip).start()
        for d in range(chips - 1):
            along_copy(s, d).start()
        return carry

    lax.fori_loop(0, sections, spread_rows, 0)

    def copies(make, slot):
        return [
            pltpu.make_async_remote_copy(
                src_ref=source,
                dst_ref=target,
                send_sem=send_sem.at[slot, d],
                recv_sem=recv_sem.at[slot, d],
                device_id={"section": peers[d]},
                device_id_type=pl.DeviceIdType.MESH,
            )
            for d in range(sections - 1)
            for source, target in [make(d)]
        ]

    def to_owners(step):
        def make(d):
            rows = pl.ds(pl.multiple_of(peers[d] * block, block), block)
            return outgoing.at[step, rows], landed.at[step, d]

        return copies(make, 2 * step)

    def to_all(ref, s, step):
        def make(d):
            return ref.at[s, own], ref.at[s, own]

        return copies(make, 2 * step + 1)

    def start(sent):
        for copy in sent:
            copy.start()

    def arrived(sent):
        for copy in sent:
            copy.wait_recv()

    joint[...] = jnp.zeros_like(joint)
    for load in loads:
        load.wait()
    usable = owners_ref[:, :1]
    for user in range(1, USERS_DEV):
        usable = usable + owners_ref[:, user : user + 1]
    grad_out[sections - 1] = (grad_out[sections - 1].astype(jnp.float32) * usable).astype(
        jnp.bfloat16
    )

    def forward(s, carry):
        for d in range(chips - 1):
            along_copy(s, d).wait_recv()
            sibling_copy(s, d + 1, behind[d]).start()
        for slot in range(chips):
            sibling_copy(s, slot, chip).wait_recv()
        widened = hidden[s].astype(jnp.float32)
        now = (widened * gains[s]).astype(jnp.bfloat16)
        scaled[s] = now
        product = jnp.dot(now, low[s, 0], preferred_element_type=jnp.float32)
        square = jnp.sum(widened * widened, axis=-1, keepdims=True)
        own_part[:, :width] = product
        own_part[:, width:] = jnp.broadcast_to(square, (tok_rows, LANES))
        outgoing[s, :, :width] = product.astype(jnp.bfloat16)
        outgoing[s, :, width:] = split_lanes(square, tok_rows)
        sent = to_owners(s)
        start(sent)
        arrived(sent)
        total = own_part[own, :width]
        mean = own_part[own, width : width + 1]
        for d in range(sections - 1):
            piece = landed[s, d]
            total = total + piece[:, :width].astype(jnp.float32)
            mean = mean + joined_lanes(piece, width)
        scale = lax.rsqrt(mean / model_width + NORM_EPS)
        value = total * scale
        inner[s] = value
        inverse[s] = jnp.broadcast_to(scale, (block, LANES))
        active[s, own] = (value / (1.0 + jnp.exp(-value))).astype(jnp.bfloat16)
        sent = to_all(active, s, s)
        start(sent)
        arrived(sent)

        @pl.when(s < sections - 1)
        def _():
            branch = dot_nt(active[s], low[s, 1])
            hidden[s + 1] = (hidden[s].astype(jnp.float32) + branch).astype(jnp.bfloat16)

        return carry

    lax.fori_loop(0, sections, forward, 0)

    def backward(back, carry):
        s = sections - 1 - back
        step = sections + back
        product = jnp.dot(grad_out[s], low[s, 1], preferred_element_type=jnp.float32)
        own_part[:, :width] = product
        outgoing[step, :, :width] = product.astype(jnp.bfloat16)
        sent = to_owners(step)
        start(sent)
        joint[...] += dot_nt(active[s], active[s]) * dot_nt(grad_out[s], grad_out[s])
        arrived(sent)
        total = own_part[own, :width]
        for d in range(sections - 1):
            total = total + landed[step, d, :, :width].astype(jnp.float32)
        value = inner[s]
        scale = inverse[s][:, :1]
        sigmoid_val = 1.0 / (1.0 + jnp.exp(-value))
        grad_inner = total * sigmoid_val * (1.0 + value * (1.0 - sigmoid_val))
        pull = jnp.sum(grad_inner * value, axis=-1, keepdims=True) * (
            scale * scale / model_width
        )
        grad_scaled[s, own, :width] = (grad_inner * scale).astype(jnp.bfloat16)
        grad_scaled[s, own, width:] = split_lanes(pull, block)
        sent = to_all(grad_scaled, s, step)
        start(sent)
        gram = dot_nt(scaled[s], scaled[s])
        arrived(sent)
        whole = grad_scaled[s]
        low_grad = whole[:, :width]

        @pl.when(s > 0)
        def _():
            grad_out[s - 1] = (
                grad_out[s].astype(jnp.float32)
                + gains[s] * dot_nt(low_grad, low[s, 0])
                - hidden[s].astype(jnp.float32) * joined_lanes(whole, width)
            ).astype(jnp.bfloat16)

        joint[...] += gram * dot_nt(low_grad, low_grad)
        return carry

    lax.fori_loop(0, sections, backward, 0)

    row_of = lax.broadcasted_iota(jnp.int32, (8, LANES), 0)
    sums = jnp.zeros((8, LANES), jnp.float32)
    for user in range(USERS_DEV):
        spread = joint[...] * owners_row_ref[user : user + 1, :]
        held_sum = jnp.sum(spread, axis=-1, keepdims=True) * owners_ref[:, user : user + 1]
        whole_sum = jnp.sum(held_sum, axis=0, keepdims=True)
        sums = jnp.where(row_of == user, whole_sum, sums)
    squares[me] = sums
    sent = copies(lambda d: (squares.at[me], squares.at[me]), 4 * sections)
    start(sent)
    arrived(sent)
    total = squares[0]
    for s in range(1, sections):
        total = total + squares[s]
    user_norm = jnp.sqrt(total)
    norm_ref[...] = user_norm
    factors = LOSS_SCALE / jnp.maximum(user_norm, CLIP_BOUND)
    token_factor = owners_ref[:, :1] * factors[:1, :1]
    for user in range(1, USERS_DEV):
        token_factor = token_factor + owners_ref[:, user : user + 1] * factors[user : user + 1, :1]

    def pair_copy(s):
        return remote(
            terms.at[s, 1 - core], sibling_terms.at[s], pair_send.at[s], pair_recv.at[s],
            "dp", sibling,
        )

    def chip_copy(s, d):
        return remote(
            chip_sums.at[s, ahead[d]], chip_landed.at[s, d], chip_send.at[s, d],
            chip_recv.at[s, d], "dp", ahead[d] * 2 + core,
        )

    def final_copy(target, source):
        return remote(
            final_out.at[target], final_landed.at[me], final_send.at[target],
            final_recv.at[source], "section", target,
        )

    def products(s):
        weighted_inner = (grad_scaled[s, :, :width].astype(jnp.float32) * token_factor).astype(
            jnp.bfloat16
        )
        weighted_out = (grad_out[s].astype(jnp.float32) * token_factor).astype(jnp.bfloat16)
        down = dot_tn(scaled[s], weighted_inner).astype(jnp.bfloat16)
        up = dot_tn(weighted_out, active[s]).astype(jnp.bfloat16)
        for at_chip in range(chips):
            for at_core in range(2):
                row = (at_chip * 2 + at_core) * part
                terms[s, at_core, at_chip, 0] = down[row : row + part]
                terms[s, at_core, at_chip, 1] = up[row : row + part]
        pair_copy(s).start()

    def chip_sum(s):
        pair_copy(s).wait_recv()
        chip_sums[s] = (
            terms[s, core].astype(jnp.float32) + sibling_terms[s].astype(jnp.float32)
        ).astype(jnp.bfloat16)
        for d in range(chips - 1):
            chip_copy(s, d).start()

    products(0)

    def products_step(s, carry):
        products(s)
        chip_sum(s - 1)
        return carry

    lax.fori_loop(1, sections, products_step, 0)
    chip_sum(sections - 1)

    def finish(s, carry):
        total = terms[s, core, chip].astype(jnp.float32) + sibling_terms[s, chip].astype(
            jnp.float32
        )
        for d in range(chips - 1):
            chip_copy(s, d).wait_recv()
            total = total + chip_landed[s, d].astype(jnp.float32)
        final_out[s] = total.astype(jnp.bfloat16)

        @pl.when(s != me)
        def _():
            final_copy(s, me).start()

        @pl.when(s == me)
        def _():
            final_landed[s] = final_out[s]

        return carry

    lax.fori_loop(0, sections, finish, 0)

    def collect(s, carry):
        @pl.when(s != me)
        def _():
            final_copy(s, s).wait_recv()

        gradient_ref[s] = final_landed[s]
        return carry

    lax.fori_loop(0, sections, collect, 0)

    for d in range(sections - 1):
        rows_copy(peers[d], d, me).wait_send()
        gains_copy(peers[d], d, me).wait_send()

    def drain_rows(s, carry):
        for slot in range(chips):
            sibling_copy(s, slot, chip).wait_send()
        for d in range(chips - 1):
            along_copy(s, d).wait_send()
            chip_copy(s, d).wait_send()
        pair_copy(s).wait_send()

        @pl.when(s != me)
        def _():
            final_copy(s, me).wait_send()

        return carry

    lax.fori_loop(0, sections, drain_rows, 0)

    def drain(step, carry):
        for copy in to_owners(step) + to_all(active, 0, step):
            copy.wait_send()
        return carry

    def drain_back(step, carry):
        for copy in to_owners(step) + to_all(grad_scaled, 0, step):
            copy.wait_send()
        return carry

    lax.fori_loop(0, sections, drain, 0)
    lax.fori_loop(sections, 2 * sections, drain_back, 0)
    for copy in sent:
        copy.wait_send()


def chain(tokens, cotangent, gains, owners, rows, shards, load_width, model_width):
    sections, _, part, width = rows.shape
    held = part * shards
    tok_rows = tokens.shape[0]
    block = tok_rows // sections
    chips = shards // 2
    vmem = pl.BlockSpec(memory_space=pltpu.VMEM)
    anywhere = pl.BlockSpec(memory_space=pl.ANY)
    owners_row = jnp.pad(owners.T, ((0, 8 - USERS_DEV), (0, 0)))
    owners = jnp.pad(owners, ((0, 0), (0, LANES - USERS_DEV)))
    steps = 2 * sections
    copies = (2 * steps + 1, sections - 1)
    bf16, f32 = jnp.bfloat16, jnp.float32
    dma = pltpu.SemaphoreType.DMA
    return pl.pallas_call(
        functools.partial(chain_kernel, sections, model_width, load_width),
        out_shape=(
            jax.ShapeDtypeStruct(rows.shape, bf16),
            jax.ShapeDtypeStruct((8, LANES), f32),
        ),
        in_specs=[anywhere, anywhere, vmem, vmem, vmem, vmem],
        out_specs=(vmem, vmem),
        scratch_shapes=[
            pltpu.VMEM((sections, 2, held, width), bf16),
            pltpu.VMEM((sections, 1, held), f32),
            pltpu.VMEM((sections, tok_rows, held), bf16),
            pltpu.VMEM((sections, tok_rows, held), bf16),
            pltpu.VMEM((sections, tok_rows, held), bf16),
            pltpu.VMEM((sections, tok_rows, width), bf16),
            pltpu.VMEM((sections, tok_rows, width + LANES), bf16),
            pltpu.VMEM((sections, block, width), f32),
            pltpu.VMEM((sections, block, LANES), f32),
            pltpu.VMEM((tok_rows, width + LANES), f32),
            pltpu.VMEM((steps, tok_rows, width + LANES), bf16),
            pltpu.VMEM((steps, sections - 1, block, width + LANES), bf16),
            pltpu.VMEM((tok_rows, tok_rows), f32),
            pltpu.VMEM((sections, 8, LANES), f32),
            pltpu.VMEM((sections, 2, chips, 2, part, width), bf16),
            pltpu.VMEM((sections, chips, 2, part, width), bf16),
            pltpu.VMEM((sections, chips, 2, part, width), bf16),
            pltpu.VMEM((sections, chips - 1, 2, part, width), bf16),
            pltpu.VMEM((sections, 2, part, width), bf16),
            pltpu.VMEM((sections, 2, part, width), bf16),
            dma(copies),
            dma(copies),
            dma((2, held // load_width)),
            dma((sections - 1,)),
            dma((sections,)),
            dma((sections - 1,)),
            dma((sections,)),
            dma((sections, chips - 1)),
            dma((sections, chips - 1)),
            dma((sections, chips)),
            dma((sections, chips)),
            dma((sections,)),
            dma((sections,)),
            dma((sections, chips - 1)),
            dma((sections, chips - 1)),
            dma((sections,)),
            dma((sections,)),
        ],
        compiler_params=pltpu.CompilerParams(
            collective_id=0, has_side_effects=True, vmem_limit_bytes=52 * 1024 * 1024
        ),
    )(tokens, cotangent, gains, owners, owners_row, rows)


def on_device(
    tokens, cotangent, lengths, seq_user, norm_gains, weights, first_moment, second_moment
):
    sections = lax.axis_size("section")
    quarter = lax.axis_index("section")
    shards = lax.axis_size("dp")
    tok_rows, model_width = tokens.shape
    own_rows, _, width = weights.shape[1:]
    part = own_rows // sections
    held = shards * part

    def own_features(values):
        split = values.reshape(tok_rows, shards, sections, part)
        return lax.dynamic_index_in_dim(split, quarter, 2, keepdims=False).reshape(tok_rows, held)

    low = weights[0].astype(jnp.bfloat16).reshape(sections, part, 2, width)
    low = low.transpose(0, 2, 1, 3)
    gains = norm_gains[0].reshape(shards, sections, part).transpose(1, 0, 2)
    gains = gains.reshape(sections, 1, held)

    positions = jnp.arange(tok_rows) % SEQLEN
    usable = positions < jnp.repeat(lengths, SEQLEN)
    local_user = seq_user - lax.axis_index("dp") * USERS_DEV
    token_user = jnp.repeat(local_user, SEQLEN)
    owners = ((token_user[:, None] == jnp.arange(USERS_DEV)[None, :]) & usable[:, None]).astype(
        jnp.float32
    )

    load_width = part
    if part % LANES != 0:
        tokens, cotangent, load_width = own_features(tokens), own_features(cotangent), held
    gradient, norms = chain(
        tokens, cotangent, gains, owners, low, shards, load_width, model_width
    )
    user_norm = norms[:USERS_DEV, 0]
    gradient = gradient.transpose(0, 2, 1, 3).reshape(own_rows, 2, width).astype(jnp.float32)
    moment_one = BETA_ONE * first_moment[0] + (1.0 - BETA_ONE) * gradient
    moment_two = BETA_TWO * second_moment[0] + (1.0 - BETA_TWO) * gradient * gradient
    direction = moment_one / FIRST_FIX / (jnp.sqrt(moment_two / SECOND_FIX) + ADAM_EPS)
    return (moment_one[None], moment_two[None], direction[None], user_norm / CLIP_BOUND)


def solution(mesh):
    return jax.shard_map(
        on_device,
        mesh=mesh,
        in_specs=(
            P("dp", None),
            P("dp", None),
            P("dp"),
            P("dp"),
            P("section", None),
            P("section", "dp", None, None),
            P("section", "dp", None, None),
            P("section", "dp", None, None),
        ),
        out_specs=(
            P("section", "dp", None, None),
            P("section", "dp", None, None),
            P("section", "dp", None, None),
            P("dp"),
        ),
        check_vma=False,
    )
```

```python
import functools

import jax
import jax.numpy as jnp
from jax import lax
from jax.experimental import pallas as pl
from jax.experimental.pallas import tpu as pltpu
from jax.sharding import PartitionSpec as P

SEQLEN = 64
USERS_DEV = 2


CLIP_BOUND = 70000.0
LOSS_SCALE = 1024.0
BETA_ONE = 0.9
BETA_TWO = 0.999
FIRST_FIX = 1.0 - 0.9**50
SECOND_FIX = 1.0 - 0.999**50
ADAM_EPS = 1e-08
NORM_EPS = 1e-05
LANES = 128


def dot_nt(left, right):
    return lax.dot_general(
        left, right, (((1,), (1,)), ((), ())), preferred_element_type=jnp.float32
    )


def dot_tn(left, right):
    return lax.dot_general(
        left, right, (((0,), (0,)), ((), ())), preferred_element_type=jnp.float32
    )


def split_lanes(column, rows):
    wide = jnp.broadcast_to(column, (rows, LANES))
    high = wide.astype(jnp.bfloat16).astype(jnp.float32)
    lane = lax.broadcasted_iota(jnp.int32, (rows, LANES), 1)
    return jnp.where(lane < LANES // 2, high, wide - high).astype(jnp.bfloat16)


def joined_lanes(block, start):
    high = block[:, start : start + 1].astype(jnp.float32)
    return high + block[:, start + LANES // 2 : start + LANES // 2 + 1].astype(jnp.float32)


def chain_kernel(
    sections,
    model_width,
    load_width,
    tokens_ref,
    cotangent_ref,
    own_gains_ref,
    owners_ref,
    owners_row_ref,
    rows_ref,
    gradient_ref,
    norm_ref,
    low,
    gains,
    hidden,
    scaled,
    grad_out,
    active,
    grad_scaled,
    inner,
    inverse,
    own_part,
    outgoing,
    landed,
    joint,
    squares,
    terms,
    sibling_terms,
    chip_sums,
    chip_landed,
    final_out,
    final_landed,
    relay_landed,
    total_ref,
    send_sem,
    recv_sem,
    load_sem,
    rows_send,
    rows_recv,
    gains_send,
    gains_recv,
    along_send,
    along_recv,
    sibling_send,
    sibling_recv,
    pair_send,
    pair_recv,
    chip_send,
    chip_recv,
    final_send,
    final_recv,
    onward_send,
    relay_send,
    relay_recv,
):
    me = lax.axis_index("section")
    place = lax.axis_index("dp")
    chips = lax.axis_size("dp") // 2
    chip, core = place // 2, lax.rem(place, 2)
    sibling = chip * 2 + 1 - core
    _, tok_rows, held = hidden.shape
    width = active.shape[2]
    part = rows_ref.shape[2]
    block = tok_rows // sections
    own = pl.ds(pl.multiple_of(me * block, block), block)
    peers = [lax.rem(me + d, sections) for d in range(1, sections)]

    barrier = pltpu.get_barrier_semaphore()
    for peer in peers:
        pl.semaphore_signal(
            barrier, inc=1, device_id={"section": peer}, device_id_type=pl.DeviceIdType.MESH
        )
    ahead = [lax.rem(chip + d, chips) for d in range(1, chips)]
    behind = [lax.rem(chip + chips - d, chips) for d in range(1, chips)]
    for other in [sibling] + [a * 2 + core for a in ahead]:
        pl.semaphore_signal(
            barrier, inc=1, device_id={"dp": other}, device_id_type=pl.DeviceIdType.MESH
        )
    pl.semaphore_wait(barrier, sections - 1 + chips)

    def remote(source, target, sent, received, axis, index):
        return pltpu.make_async_remote_copy(
            src_ref=source,
            dst_ref=target,
            send_sem=sent,
            recv_sem=received,
            device_id={axis: index},
            device_id_type=pl.DeviceIdType.MESH,
        )

    def shard(s, at_chip, at_core):
        row = pl.multiple_of((at_chip * 2 + at_core) * part, part)
        return low.at[s, :, pl.ds(row, part)]

    pieces = held // load_width
    loads = []
    for which, (source, target) in enumerate(
        ((tokens_ref, hidden.at[0]), (cotangent_ref, grad_out.at[sections - 1]))
    ):
        for piece in range(pieces):
            first = (piece * sections + me) * load_width if pieces > 1 else 0
            loads.append(
                pltpu.make_async_copy(
                    source.at[:, pl.ds(pl.multiple_of(first, load_width), load_width)],
                    target.at[:, pl.ds(piece * load_width, load_width)],
                    load_sem.at[which, piece],
                )
            )

    def rows_copy(target, slot, source):
        return remote(
            rows_ref.at[target], shard(me, chip, core), rows_send.at[slot], rows_recv.at[source],
            "section", target,
        )

    def gains_copy(target, slot, source):
        return remote(
            own_gains_ref.at[target], gains.at[me], gains_send.at[slot], gains_recv.at[source],
            "section", target,
        )

    def along_copy(s, d):
        return remote(
            shard(s, chip, core), shard(s, chip, core), along_send.at[s, d], along_recv.at[s, d],
            "dp", ahead[d] * 2 + core,
        )

    def sibling_copy(s, slot, at_chip):
        return remote(
            shard(s, at_chip, core), shard(s, at_chip, core),
            sibling_send.at[s, slot], sibling_recv.at[s, slot], "dp", sibling,
        )

    for d in range(sections - 1):
        rows_copy(peers[d], d, me).start()
        gains_copy(peers[d], d, me).start()
    for load in loads:
        load.start()
    low[me, :, pl.ds(pl.multiple_of(place * part, part), part)] = rows_ref[me]
    gains[me] = own_gains_ref[me]

    last = chips - 1
    relayed = chips >= 4

    def when_not(excluded, run):
        if not excluded:
            run()
            return
        allowed = chip != excluded[0]
        for other in excluded[1:]:
            allowed = allowed & (chip != other)
        pl.when(allowed)(run)

    def not_sent(d):
        return [c for c, at in ((0, chips - 2), (last, 0)) if relayed and d == at]

    def held_back(d):
        return [c for c, at in ((1, chips - 3), (last - 1, 1)) if relayed and d == at]

    def not_received(d):
        return [c for c, at in ((last, chips - 2), (0, 0)) if relayed and d == at]

    def spread_rows(s):
        @pl.when(s != me)
        def _():
            rows_copy(peers[0], 0, s).wait_recv()
            gains_copy(peers[0], 0, s).wait_recv()

        sibling_copy(s, 0, chip).start()
        for d in range(chips - 1):
            when_not(not_sent(d), along_copy(s, d).start)

    def rows_left(s):
        for d in range(chips - 1):
            when_not(not_sent(d), along_copy(s, d).wait_send)

    def onward_high(s):
        return remote(
            shard(s, 0, core), shard(s, 0, core), onward_send.at[s],
            along_recv.at[s, chips - 2], "dp", last * 2 + core,
        )

    def onward_low(s):
        return remote(
            shard(s, last, core), shard(s, last, core), onward_send.at[s],
            along_recv.at[s, 0], "dp", core,
        )

    spread_rows(0)
    rows_left(0)
    spread_rows(1)

    def copies(make, slot):
        return [
            pltpu.make_async_remote_copy(
                src_ref=source,
                dst_ref=target,
                send_sem=send_sem.at[slot, d],
                recv_sem=recv_sem.at[slot, d],
                device_id={"section": peers[d]},
                device_id_type=pl.DeviceIdType.MESH,
            )
            for d in range(sections - 1)
            for source, target in [make(d)]
        ]

    def to_owners(step):
        def make(d):
            rows = pl.ds(pl.multiple_of(peers[d] * block, block), block)
            return outgoing.at[step, rows], landed.at[step, d]

        return copies(make, 2 * step)

    def to_all(ref, s, step):
        def make(d):
            return ref.at[s, own], ref.at[s, own]

        return copies(make, 2 * step + 1)

    def start(sent):
        for copy in sent:
            copy.start()

    def arrived(sent):
        for copy in sent:
            copy.wait_recv()

    joint[...] = jnp.zeros_like(joint)
    for load in loads:
        load.wait()
    usable = owners_ref[:, :1]
    for user in range(1, USERS_DEV):
        usable = usable + owners_ref[:, user : user + 1]
    grad_out[sections - 1] = (grad_out[sections - 1].astype(jnp.float32) * usable).astype(
        jnp.bfloat16
    )

    def forward(s, carry):
        for d in [*range(1, chips - 2), 0, chips - 2] if relayed else range(chips - 1):
            along_copy(s, d).wait_recv()
            if relayed and d == chips - 3:
                pl.when(chip == last - 1)(onward_high(s).start)
            if relayed and d == 1:
                pl.when(chip == 1)(onward_low(s).start)
            sibling_copy(s, d + 1, behind[d]).start()
        for slot in range(chips):
            sibling_copy(s, slot, chip).wait_recv()
        widened = hidden[s].astype(jnp.float32)
        now = (widened * gains[s]).astype(jnp.bfloat16)
        scaled[s] = now
        product = jnp.dot(now, low[s, 0], preferred_element_type=jnp.float32)
        square = jnp.sum(widened * widened, axis=-1, keepdims=True)
        own_part[:, :width] = product
        own_part[:, width:] = jnp.broadcast_to(square, (tok_rows, LANES))
        outgoing[s, :, :width] = product.astype(jnp.bfloat16)
        outgoing[s, :, width:] = split_lanes(square, tok_rows)
        sent = to_owners(s)
        start(sent)

        @pl.when(s + 2 < sections)
        def _():
            rows_left(s + 1)
            spread_rows(s + 2)

        arrived(sent)
        total = own_part[own, :width]
        mean = own_part[own, width : width + 1]
        for d in range(sections - 1):
            piece = landed[s, d]
            total = total + piece[:, :width].astype(jnp.float32)
            mean = mean + joined_lanes(piece, width)
        scale = lax.rsqrt(mean / model_width + NORM_EPS)
        value = total * scale
        inner[s] = value
        inverse[s] = jnp.broadcast_to(scale, (block, LANES))
        active[s, own] = (value / (1.0 + jnp.exp(-value))).astype(jnp.bfloat16)
        sent = to_all(active, s, s)
        start(sent)
        arrived(sent)

        @pl.when(s < sections - 1)
        def _():
            branch = dot_nt(active[s], low[s, 1])
            hidden[s + 1] = (hidden[s].astype(jnp.float32) + branch).astype(jnp.bfloat16)

        return carry

    lax.fori_loop(0, sections, forward, 0)

    def backward(back, carry):
        s = sections - 1 - back
        step = sections + back
        product = jnp.dot(grad_out[s], low[s, 1], preferred_element_type=jnp.float32)
        own_part[:, :width] = product
        outgoing[step, :, :width] = product.astype(jnp.bfloat16)
        sent = to_owners(step)
        start(sent)
        joint[...] += dot_nt(active[s], active[s]) * dot_nt(grad_out[s], grad_out[s])
        arrived(sent)
        total = own_part[own, :width]
        for d in range(sections - 1):
            total = total + landed[step, d, :, :width].astype(jnp.float32)
        value = inner[s]
        scale = inverse[s][:, :1]
        sigmoid_val = 1.0 / (1.0 + jnp.exp(-value))
        grad_inner = total * sigmoid_val * (1.0 + value * (1.0 - sigmoid_val))
        pull = jnp.sum(grad_inner * value, axis=-1, keepdims=True) * (
            scale * scale / model_width
        )
        grad_scaled[s, own, :width] = (grad_inner * scale).astype(jnp.bfloat16)
        grad_scaled[s, own, width:] = split_lanes(pull, block)
        sent = to_all(grad_scaled, s, step)
        start(sent)
        gram = dot_nt(scaled[s], scaled[s])
        arrived(sent)
        whole = grad_scaled[s]
        low_grad = whole[:, :width]

        @pl.when(s > 0)
        def _():
            grad_out[s - 1] = (
                grad_out[s].astype(jnp.float32)
                + gains[s] * dot_nt(low_grad, low[s, 0])
                - hidden[s].astype(jnp.float32) * joined_lanes(whole, width)
            ).astype(jnp.bfloat16)

        joint[...] += gram * dot_nt(low_grad, low_grad)
        return carry

    lax.fori_loop(0, sections, backward, 0)

    row_of = lax.broadcasted_iota(jnp.int32, (8, LANES), 0)
    sums = jnp.zeros((8, LANES), jnp.float32)
    for user in range(USERS_DEV):
        spread = joint[...] * owners_row_ref[user : user + 1, :]
        held_sum = jnp.sum(spread, axis=-1, keepdims=True) * owners_ref[:, user : user + 1]
        whole_sum = jnp.sum(held_sum, axis=0, keepdims=True)
        sums = jnp.where(row_of == user, whole_sum, sums)
    squares[me] = sums
    sent = copies(lambda d: (squares.at[me], squares.at[me]), 4 * sections)
    start(sent)
    arrived(sent)
    total = squares[0]
    for s in range(1, sections):
        total = total + squares[s]
    user_norm = jnp.sqrt(total)
    norm_ref[...] = user_norm
    factors = LOSS_SCALE / jnp.maximum(user_norm, CLIP_BOUND)
    token_factor = owners_ref[:, :1] * factors[:1, :1]
    for user in range(1, USERS_DEV):
        token_factor = token_factor + owners_ref[:, user : user + 1] * factors[user : user + 1, :1]

    def pair_copy(s):
        return remote(
            terms.at[s, 1 - core], sibling_terms.at[s], pair_send.at[s], pair_recv.at[s],
            "dp", sibling,
        )

    def chip_copy(s, d):
        return remote(
            chip_sums.at[s, ahead[d]], chip_landed.at[s, d], chip_send.at[s, d],
            chip_recv.at[s, d], "dp", ahead[d] * 2 + core,
        )

    def final_copy(target, source):
        return remote(
            final_out.at[target], final_landed.at[me], final_send.at[target],
            final_recv.at[source], "section", target,
        )

    def products(s):
        weighted_inner = (grad_scaled[s, :, :width].astype(jnp.float32) * token_factor).astype(
            jnp.bfloat16
        )
        weighted_out = (grad_out[s].astype(jnp.float32) * token_factor).astype(jnp.bfloat16)
        down = dot_tn(scaled[s], weighted_inner).astype(jnp.bfloat16)
        up = dot_tn(weighted_out, active[s]).astype(jnp.bfloat16)
        for at_chip in range(chips):
            for at_core in range(2):
                row = (at_chip * 2 + at_core) * part
                terms[s, at_core, at_chip, 0] = down[row : row + part]
                terms[s, at_core, at_chip, 1] = up[row : row + part]
        pair_copy(s).start()

    def chip_sum(s):
        pair_copy(s).wait_recv()
        chip_sums[s] = (
            terms[s, core].astype(jnp.float32) + sibling_terms[s].astype(jnp.float32)
        ).astype(jnp.bfloat16)
        for d in range(chips - 1):
            when_not(not_sent(d) + held_back(d), chip_copy(s, d).start)
        if relayed:
            pl.when(chip == 0)(from_low(s).start)
            pl.when(chip == last)(from_high(s).start)

    def from_low(s):
        return remote(
            chip_sums.at[s, last], relay_landed.at[s], relay_send.at[s], relay_recv.at[s],
            "dp", 2 + core,
        )

    def from_high(s):
        return remote(
            chip_sums.at[s, 0], relay_landed.at[s], relay_send.at[s], relay_recv.at[s],
            "dp", (last - 1) * 2 + core,
        )

    def add_relayed(s, target):
        from_low(s).wait_recv()
        chip_sums[s, target] = (
            chip_sums[s, target].astype(jnp.float32) + relay_landed[s].astype(jnp.float32)
        ).astype(jnp.bfloat16)

    def relay_sum(s):
        if not relayed:
            return

        @pl.when(chip == 1)
        def _():
            add_relayed(s, last)
            chip_copy(s, chips - 3).start()

        @pl.when(chip == last - 1)
        def _():
            add_relayed(s, 0)
            chip_copy(s, 1).start()

    products(0)
    products(1)
    chip_sum(0)

    def products_step(s, carry):
        products(s)
        chip_sum(s - 1)
        relay_sum(s - 2)
        return carry

    lax.fori_loop(2, sections, products_step, 0)
    chip_sum(sections - 1)
    relay_sum(sections - 2)
    relay_sum(sections - 1)

    def finish(s, carry):
        total_ref[...] = terms[s, core, chip].astype(jnp.float32) + sibling_terms[
            s, chip
        ].astype(jnp.float32)
        for d in range(chips - 1):

            def add(d=d):
                chip_copy(s, d).wait_recv()
                total_ref[...] += chip_landed[s, d].astype(jnp.float32)

            when_not(not_received(d), add)
        final_out[s] = total_ref[...].astype(jnp.bfloat16)

        @pl.when(s != me)
        def _():
            final_copy(s, me).start()

        @pl.when(s == me)
        def _():
            final_landed[s] = final_out[s]

        return carry

    lax.fori_loop(0, sections, finish, 0)

    def collect(s, carry):
        @pl.when(s != me)
        def _():
            final_copy(s, s).wait_recv()

        gradient_ref[s] = final_landed[s]
        return carry

    lax.fori_loop(0, sections, collect, 0)

    for d in range(sections - 1):
        rows_copy(peers[d], d, me).wait_send()
        gains_copy(peers[d], d, me).wait_send()

    def drain_rows(s, carry):
        for slot in range(chips):
            sibling_copy(s, slot, chip).wait_send()
        for d in range(chips - 1):
            when_not(not_sent(d), chip_copy(s, d).wait_send)
        if relayed:
            pl.when((chip == 1) | (chip == last - 1))(onward_high(s).wait_send)
            pl.when((chip == 0) | (chip == last))(from_low(s).wait_send)
        pair_copy(s).wait_send()

        @pl.when(s != me)
        def _():
            final_copy(s, me).wait_send()

        return carry

    rows_left(sections - 1)
    lax.fori_loop(0, sections, drain_rows, 0)

    def drain(step, carry):
        for copy in to_owners(step) + to_all(active, 0, step):
            copy.wait_send()
        return carry

    def drain_back(step, carry):
        for copy in to_owners(step) + to_all(grad_scaled, 0, step):
            copy.wait_send()
        return carry

    lax.fori_loop(0, sections, drain, 0)
    lax.fori_loop(sections, 2 * sections, drain_back, 0)
    for copy in sent:
        copy.wait_send()


def chain(tokens, cotangent, gains, owners, rows, shards, load_width, model_width):
    sections, _, part, width = rows.shape
    held = part * shards
    tok_rows = tokens.shape[0]
    block = tok_rows // sections
    chips = shards // 2
    vmem = pl.BlockSpec(memory_space=pltpu.VMEM)
    anywhere = pl.BlockSpec(memory_space=pl.ANY)
    owners_row = jnp.pad(owners.T, ((0, 8 - USERS_DEV), (0, 0)))
    owners = jnp.pad(owners, ((0, 0), (0, LANES - USERS_DEV)))
    steps = 2 * sections
    copies = (2 * steps + 1, sections - 1)
    bf16, f32 = jnp.bfloat16, jnp.float32
    dma = pltpu.SemaphoreType.DMA
    return pl.pallas_call(
        functools.partial(chain_kernel, sections, model_width, load_width),
        out_shape=(
            jax.ShapeDtypeStruct(rows.shape, bf16),
            jax.ShapeDtypeStruct((8, LANES), f32),
        ),
        in_specs=[anywhere, anywhere, vmem, vmem, vmem, vmem],
        out_specs=(vmem, vmem),
        scratch_shapes=[
            pltpu.VMEM((sections, 2, held, width), bf16),
            pltpu.VMEM((sections, 1, held), f32),
            pltpu.VMEM((sections, tok_rows, held), bf16),
            pltpu.VMEM((sections, tok_rows, held), bf16),
            pltpu.VMEM((sections, tok_rows, held), bf16),
            pltpu.VMEM((sections, tok_rows, width), bf16),
            pltpu.VMEM((sections, tok_rows, width + LANES), bf16),
            pltpu.VMEM((sections, block, width), f32),
            pltpu.VMEM((sections, block, LANES), f32),
            pltpu.VMEM((tok_rows, width + LANES), f32),
            pltpu.VMEM((steps, tok_rows, width + LANES), bf16),
            pltpu.VMEM((steps, sections - 1, block, width + LANES), bf16),
            pltpu.VMEM((tok_rows, tok_rows), f32),
            pltpu.VMEM((sections, 8, LANES), f32),
            pltpu.VMEM((sections, 2, chips, 2, part, width), bf16),
            pltpu.VMEM((sections, chips, 2, part, width), bf16),
            pltpu.VMEM((sections, chips, 2, part, width), bf16),
            pltpu.VMEM((sections, chips - 1, 2, part, width), bf16),
            pltpu.VMEM((sections, 2, part, width), bf16),
            pltpu.VMEM((sections, 2, part, width), bf16),
            pltpu.VMEM((sections, 2, part, width), bf16),
            pltpu.VMEM((2, part, width), f32),
            dma(copies),
            dma(copies),
            dma((2, held // load_width)),
            dma((sections - 1,)),
            dma((sections,)),
            dma((sections - 1,)),
            dma((sections,)),
            dma((sections, chips - 1)),
            dma((sections, chips - 1)),
            dma((sections, chips)),
            dma((sections, chips)),
            dma((sections,)),
            dma((sections,)),
            dma((sections, chips - 1)),
            dma((sections, chips - 1)),
            dma((sections,)),
            dma((sections,)),
            dma((sections,)),
            dma((sections,)),
            dma((sections,)),
        ],
        compiler_params=pltpu.CompilerParams(
            collective_id=0, has_side_effects=True, vmem_limit_bytes=52 * 1024 * 1024
        ),
    )(tokens, cotangent, gains, owners, owners_row, rows)


def on_device(
    tokens, cotangent, lengths, seq_user, norm_gains, weights, first_moment, second_moment
):
    sections = lax.axis_size("section")
    quarter = lax.axis_index("section")
    shards = lax.axis_size("dp")
    tok_rows, model_width = tokens.shape
    own_rows, _, width = weights.shape[1:]
    part = own_rows // sections
    held = shards * part

    def own_features(values):
        split = values.reshape(tok_rows, shards, sections, part)
        return lax.dynamic_index_in_dim(split, quarter, 2, keepdims=False).reshape(tok_rows, held)

    low = weights[0].astype(jnp.bfloat16).reshape(sections, part, 2, width)
    low = low.transpose(0, 2, 1, 3)
    gains = norm_gains[0].reshape(shards, sections, part).transpose(1, 0, 2)
    gains = gains.reshape(sections, 1, held)

    positions = jnp.arange(tok_rows) % SEQLEN
    usable = positions < jnp.repeat(lengths, SEQLEN)
    local_user = seq_user - lax.axis_index("dp") * USERS_DEV
    token_user = jnp.repeat(local_user, SEQLEN)
    owners = ((token_user[:, None] == jnp.arange(USERS_DEV)[None, :]) & usable[:, None]).astype(
        jnp.float32
    )

    load_width = part
    if part % LANES != 0:
        tokens, cotangent, load_width = own_features(tokens), own_features(cotangent), held
    gradient, norms = chain(
        tokens, cotangent, gains, owners, low, shards, load_width, model_width
    )
    user_norm = norms[:USERS_DEV, 0]
    gradient = gradient.transpose(0, 2, 1, 3).reshape(own_rows, 2, width).astype(jnp.float32)
    moment_one = BETA_ONE * first_moment[0] + (1.0 - BETA_ONE) * gradient
    moment_two = BETA_TWO * second_moment[0] + (1.0 - BETA_TWO) * gradient * gradient
    direction = moment_one / FIRST_FIX / (jnp.sqrt(moment_two / SECOND_FIX) + ADAM_EPS)
    return (moment_one[None], moment_two[None], direction[None], user_norm / CLIP_BOUND)


def solution(mesh):
    return jax.shard_map(
        on_device,
        mesh=mesh,
        in_specs=(
            P("dp", None),
            P("dp", None),
            P("dp"),
            P("dp"),
            P("section", None),
            P("section", "dp", None, None),
            P("section", "dp", None, None),
            P("section", "dp", None, None),
        ),
        out_specs=(
            P("section", "dp", None, None),
            P("section", "dp", None, None),
            P("section", "dp", None, None),
            P("dp"),
        ),
        check_vma=False,
    )
```

```python
import functools

import jax
import jax.numpy as jnp
from jax import lax
from jax.experimental import pallas as pl
from jax.experimental.layout import Layout, with_layout_constraint
from jax.experimental.pallas import tpu as pltpu
from jax.sharding import PartitionSpec as P

SEQLEN = 64
USERS_DEV = 2


CLIP_BOUND = 70000.0
LOSS_SCALE = 1024.0
BETA_ONE = 0.9
BETA_TWO = 0.999
FIRST_FIX = 1.0 - 0.9**50
SECOND_FIX = 1.0 - 0.999**50
ADAM_EPS = 1e-08
NORM_EPS = 1e-05
LANES = 128
HALVES = 2


def dot_nt(left, right):
    return lax.dot_general(
        left, right, (((1,), (1,)), ((), ())), preferred_element_type=jnp.float32
    )


def dot_tn(left, right):
    return lax.dot_general(
        left, right, (((0,), (0,)), ((), ())), preferred_element_type=jnp.float32
    )


def split_lanes(column, rows):
    wide = jnp.broadcast_to(column, (rows, LANES))
    high = wide.astype(jnp.bfloat16).astype(jnp.float32)
    lane = lax.broadcasted_iota(jnp.int32, (rows, LANES), 1)
    return jnp.where(lane < LANES // 2, high, wide - high).astype(jnp.bfloat16)


def joined_lanes(block, start):
    high = block[:, start : start + 1].astype(jnp.float32)
    return high + block[:, start + LANES // 2 : start + LANES // 2 + 1].astype(jnp.float32)


def chain_kernel(
    sections,
    model_width,
    load_width,
    tokens_ref,
    cotangent_ref,
    own_gains_ref,
    owners_ref,
    owners_row_ref,
    rows_ref,
    gradient_ref,
    norm_ref,
    low,
    gains,
    hidden,
    scaled,
    grad_out,
    active,
    grad_scaled,
    inner,
    inverse,
    own_part,
    outgoing,
    landed,
    joint,
    squares,
    terms,
    sibling_terms,
    chip_sums,
    chip_landed,
    final_out,
    final_landed,
    relay_landed,
    total_ref,
    send_sem,
    recv_sem,
    load_sem,
    rows_send,
    rows_recv,
    gains_send,
    gains_recv,
    along_send,
    along_recv,
    sibling_send,
    sibling_recv,
    pair_send,
    pair_recv,
    chip_send,
    chip_recv,
    final_send,
    final_recv,
    onward_send,
    relay_send,
    relay_recv,
):
    me = lax.axis_index("section")
    place = lax.axis_index("dp")
    chips = lax.axis_size("dp") // 2
    chip, core = place // 2, lax.rem(place, 2)
    sibling = chip * 2 + 1 - core
    _, tok_rows, held = hidden.shape
    width = active.shape[2]
    part = rows_ref.shape[2]
    half = tok_rows // HALVES
    block = half // sections
    whole = [pl.ds(h * half, half) for h in range(HALVES)]
    mine = [pl.ds(h * block, block) for h in range(HALVES)]
    peers = [lax.rem(me + d, sections) for d in range(1, sections)]

    barrier = pltpu.get_barrier_semaphore()
    for peer in peers:
        pl.semaphore_signal(
            barrier, inc=1, device_id={"section": peer}, device_id_type=pl.DeviceIdType.MESH
        )
    ahead = [lax.rem(chip + d, chips) for d in range(1, chips)]
    behind = [lax.rem(chip + chips - d, chips) for d in range(1, chips)]
    for other in [sibling] + [a * 2 + core for a in ahead]:
        pl.semaphore_signal(
            barrier, inc=1, device_id={"dp": other}, device_id_type=pl.DeviceIdType.MESH
        )
    pl.semaphore_wait(barrier, sections - 1 + chips)

    def remote(source, target, sent, received, axis, index):
        return pltpu.make_async_remote_copy(
            src_ref=source,
            dst_ref=target,
            send_sem=sent,
            recv_sem=received,
            device_id={axis: index},
            device_id_type=pl.DeviceIdType.MESH,
        )

    def shard(s, at_chip, at_core):
        row = pl.multiple_of((at_chip * 2 + at_core) * part, part)
        return low.at[s, :, pl.ds(row, part)]

    pieces = held // load_width
    loads = []
    for which, (source, target) in enumerate(
        ((tokens_ref, hidden.at[0]), (cotangent_ref, grad_out.at[sections - 1]))
    ):
        for piece in range(pieces):
            first = (piece * sections + me) * load_width if pieces > 1 else 0
            loads.append(
                pltpu.make_async_copy(
                    source.at[:, pl.ds(pl.multiple_of(first, load_width), load_width)],
                    target.at[:, pl.ds(piece * load_width, load_width)],
                    load_sem.at[which, piece],
                )
            )

    def rows_copy(target, slot, source):
        return remote(
            rows_ref.at[target], shard(me, chip, core), rows_send.at[slot], rows_recv.at[source],
            "section", target,
        )

    def gains_copy(target, slot, source):
        return remote(
            own_gains_ref.at[target], gains.at[me], gains_send.at[slot], gains_recv.at[source],
            "section", target,
        )

    def along_copy(s, d):
        return remote(
            shard(s, chip, core), shard(s, chip, core), along_send.at[s, d], along_recv.at[s, d],
            "dp", ahead[d] * 2 + core,
        )

    def sibling_copy(s, slot, at_chip):
        return remote(
            shard(s, at_chip, core), shard(s, at_chip, core),
            sibling_send.at[s, slot], sibling_recv.at[s, slot], "dp", sibling,
        )

    for d in range(sections - 1):
        rows_copy(peers[d], d, me).start()
        gains_copy(peers[d], d, me).start()
    for load in loads:
        load.start()
    low[me, :, pl.ds(pl.multiple_of(place * part, part), part)] = rows_ref[me]
    gains[me] = own_gains_ref[me]

    last = chips - 1
    relayed = chips >= 4

    def when_not(excluded, run):
        if not excluded:
            run()
            return
        allowed = chip != excluded[0]
        for other in excluded[1:]:
            allowed = allowed & (chip != other)
        pl.when(allowed)(run)

    def not_sent(d):
        return [c for c, at in ((0, chips - 2), (last, 0)) if relayed and d == at]

    def held_back(d):
        return [c for c, at in ((1, chips - 3), (last - 1, 1)) if relayed and d == at]

    def not_received(d):
        return [c for c, at in ((last, chips - 2), (0, 0)) if relayed and d == at]

    def spread_rows(s):
        @pl.when(s != me)
        def _():
            rows_copy(peers[0], 0, s).wait_recv()
            gains_copy(peers[0], 0, s).wait_recv()

        sibling_copy(s, 0, chip).start()
        for d in range(chips - 1):
            when_not(not_sent(d), along_copy(s, d).start)

    def rows_left(s):
        for d in range(chips - 1):
            when_not(not_sent(d), along_copy(s, d).wait_send)

    def onward_high(s):
        return remote(
            shard(s, 0, core), shard(s, 0, core), onward_send.at[s],
            along_recv.at[s, chips - 2], "dp", last * 2 + core,
        )

    def onward_low(s):
        return remote(
            shard(s, last, core), shard(s, last, core), onward_send.at[s],
            along_recv.at[s, 0], "dp", core,
        )

    spread_rows(0)
    rows_left(0)
    spread_rows(1)

    def copies(make, slot):
        return [
            pltpu.make_async_remote_copy(
                src_ref=source,
                dst_ref=target,
                send_sem=send_sem.at[slot, d],
                recv_sem=recv_sem.at[slot, d],
                device_id={"section": peers[d]},
                device_id_type=pl.DeviceIdType.MESH,
            )
            for d in range(sections - 1)
            for source, target in [make(d)]
        ]

    def block_of(h, index):
        return pl.ds(pl.multiple_of(h * half + index * block, block), block)

    def to_owners(step, h):
        def make(d):
            return outgoing.at[step, block_of(h, peers[d])], landed.at[step, d, mine[h]]

        return copies(make, 2 * step * HALVES + h)

    def to_all(ref, s, step, h):
        def make(d):
            return ref.at[s, block_of(h, me)], ref.at[s, block_of(h, me)]

        return copies(make, (2 * step + 1) * HALVES + h)

    def start(sent):
        for copy in sent:
            copy.start()

    def arrived(sent):
        for copy in sent:
            copy.wait_recv()

    joint[...] = jnp.zeros_like(joint)
    for load in loads:
        load.wait()
    usable = owners_ref[:, :1]
    for user in range(1, USERS_DEV):
        usable = usable + owners_ref[:, user : user + 1]
    grad_out[sections - 1] = (grad_out[sections - 1].astype(jnp.float32) * usable).astype(
        jnp.bfloat16
    )

    def forward(s, carry):
        for d in [*range(1, chips - 2), 0, chips - 2] if relayed else range(chips - 1):
            along_copy(s, d).wait_recv()
            if relayed and d == chips - 3:
                pl.when(chip == last - 1)(onward_high(s).start)
            if relayed and d == 1:
                pl.when(chip == 1)(onward_low(s).start)
            sibling_copy(s, d + 1, behind[d]).start()
        for slot in range(chips):
            sibling_copy(s, slot, chip).wait_recv()
        for h in range(HALVES):

            @pl.when(s > 0)
            def _():
                arrived(to_all(active, s - 1, s - 1, h))
                branch = dot_nt(active[s - 1, whole[h]], low[s - 1, 1])
                hidden[s, whole[h]] = (
                    hidden[s - 1, whole[h]].astype(jnp.float32) + branch
                ).astype(jnp.bfloat16)

            widened = hidden[s, whole[h]].astype(jnp.float32)
            now = (widened * gains[s]).astype(jnp.bfloat16)
            scaled[s, whole[h]] = now
            product = jnp.dot(now, low[s, 0], preferred_element_type=jnp.float32)
            square = jnp.sum(widened * widened, axis=-1, keepdims=True)
            own_part[whole[h], :width] = product
            own_part[whole[h], width:] = jnp.broadcast_to(square, (half, LANES))
            outgoing[s, whole[h], :width] = product.astype(jnp.bfloat16)
            outgoing[s, whole[h], width:] = split_lanes(square, half)
            start(to_owners(s, h))

        @pl.when(s + 2 < sections)
        def _():
            rows_left(s + 1)
            spread_rows(s + 2)

        for h in range(HALVES):
            arrived(to_owners(s, h))
            total = own_part[block_of(h, me), :width]
            mean = own_part[block_of(h, me), width : width + 1]
            for d in range(sections - 1):
                piece = landed[s, d, mine[h]]
                total = total + piece[:, :width].astype(jnp.float32)
                mean = mean + joined_lanes(piece, width)
            scale = lax.rsqrt(mean / model_width + NORM_EPS)
            value = total * scale
            inner[s, mine[h]] = value
            inverse[s, mine[h]] = jnp.broadcast_to(scale, (block, LANES))
            active[s, block_of(h, me)] = (value / (1.0 + jnp.exp(-value))).astype(jnp.bfloat16)
            start(to_all(active, s, s, h))
        return carry

    lax.fori_loop(0, sections, forward, 0)
    for h in range(HALVES):
        arrived(to_all(active, sections - 1, sections - 1, h))

    def inner_gram(s):
        low_grad = grad_scaled[s, :, :width]
        joint[...] += dot_nt(scaled[s], scaled[s]) * dot_nt(low_grad, low_grad)

    def backward(back, carry):
        s = sections - 1 - back
        step = sections + back
        for h in range(HALVES):

            @pl.when(back > 0)
            def _():
                arrived(to_all(grad_scaled, s + 1, step - 1, h))
                block_in = grad_scaled[s + 1, whole[h]]
                grad_out[s, whole[h]] = (
                    grad_out[s + 1, whole[h]].astype(jnp.float32)
                    + gains[s + 1] * dot_nt(block_in[:, :width], low[s + 1, 0])
                    - hidden[s + 1, whole[h]].astype(jnp.float32) * joined_lanes(block_in, width)
                ).astype(jnp.bfloat16)

            product = jnp.dot(
                grad_out[s, whole[h]], low[s, 1], preferred_element_type=jnp.float32
            )
            own_part[whole[h], :width] = product
            outgoing[step, whole[h], :width] = product.astype(jnp.bfloat16)
            start(to_owners(step, h))

        joint[...] += dot_nt(active[s], active[s]) * dot_nt(grad_out[s], grad_out[s])
        for h in range(HALVES):
            arrived(to_owners(step, h))
            total = own_part[block_of(h, me), :width]
            for d in range(sections - 1):
                total = total + landed[step, d, mine[h], :width].astype(jnp.float32)
            value = inner[s, mine[h]]
            scale = inverse[s, mine[h]][:, :1]
            sigmoid_val = 1.0 / (1.0 + jnp.exp(-value))
            grad_inner = total * sigmoid_val * (1.0 + value * (1.0 - sigmoid_val))
            pull = jnp.sum(grad_inner * value, axis=-1, keepdims=True) * (
                scale * scale / model_width
            )
            grad_scaled[s, block_of(h, me), :width] = (grad_inner * scale).astype(jnp.bfloat16)
            grad_scaled[s, block_of(h, me), width:] = split_lanes(pull, block)
            start(to_all(grad_scaled, s, step, h))

        @pl.when(back > 0)
        def _():
            inner_gram(s + 1)

        return carry

    lax.fori_loop(0, sections, backward, 0)
    for h in range(HALVES):
        arrived(to_all(grad_scaled, 0, 2 * sections - 1, h))
    inner_gram(0)

    row_of = lax.broadcasted_iota(jnp.int32, (8, LANES), 0)
    sums = jnp.zeros((8, LANES), jnp.float32)
    for user in range(USERS_DEV):
        spread = joint[...] * owners_row_ref[user : user + 1, :]
        held_sum = jnp.sum(spread, axis=-1, keepdims=True) * owners_ref[:, user : user + 1]
        whole_sum = jnp.sum(held_sum, axis=0, keepdims=True)
        sums = jnp.where(row_of == user, whole_sum, sums)
    squares[me] = sums
    sent = copies(lambda d: (squares.at[me], squares.at[me]), 4 * sections * HALVES)
    start(sent)
    arrived(sent)
    total = squares[0]
    for s in range(1, sections):
        total = total + squares[s]
    user_norm = jnp.sqrt(total)
    norm_ref[...] = user_norm
    factors = LOSS_SCALE / jnp.maximum(user_norm, CLIP_BOUND)
    token_factor = owners_ref[:, :1] * factors[:1, :1]
    for user in range(1, USERS_DEV):
        token_factor = token_factor + owners_ref[:, user : user + 1] * factors[user : user + 1, :1]

    def pair_copy(s):
        return remote(
            terms.at[s, 1 - core], sibling_terms.at[s], pair_send.at[s], pair_recv.at[s],
            "dp", sibling,
        )

    def chip_copy(s, d):
        return remote(
            chip_sums.at[s, ahead[d]], chip_landed.at[s, d], chip_send.at[s, d],
            chip_recv.at[s, d], "dp", ahead[d] * 2 + core,
        )

    def final_copy(target, source):
        return remote(
            final_out.at[target], final_landed.at[me], final_send.at[target],
            final_recv.at[source], "section", target,
        )

    def products(s):
        weighted_inner = (grad_scaled[s, :, :width].astype(jnp.float32) * token_factor).astype(
            jnp.bfloat16
        )
        weighted_out = (grad_out[s].astype(jnp.float32) * token_factor).astype(jnp.bfloat16)
        down = dot_tn(scaled[s], weighted_inner).astype(jnp.bfloat16)
        up = dot_tn(weighted_out, active[s]).astype(jnp.bfloat16)
        for at_chip in range(chips):
            for at_core in range(2):
                row = (at_chip * 2 + at_core) * part
                terms[s, at_core, at_chip, 0] = down[row : row + part]
                terms[s, at_core, at_chip, 1] = up[row : row + part]
        pair_copy(s).start()

    def chip_sum(s):
        pair_copy(s).wait_recv()
        chip_sums[s] = (
            terms[s, core].astype(jnp.float32) + sibling_terms[s].astype(jnp.float32)
        ).astype(jnp.bfloat16)
        for d in range(chips - 1):
            when_not(not_sent(d) + held_back(d), chip_copy(s, d).start)
        if relayed:
            pl.when(chip == 0)(from_low(s).start)
            pl.when(chip == last)(from_high(s).start)

    def from_low(s):
        return remote(
            chip_sums.at[s, last], relay_landed.at[s], relay_send.at[s], relay_recv.at[s],
            "dp", 2 + core,
        )

    def from_high(s):
        return remote(
            chip_sums.at[s, 0], relay_landed.at[s], relay_send.at[s], relay_recv.at[s],
            "dp", (last - 1) * 2 + core,
        )

    def add_relayed(s, target):
        from_low(s).wait_recv()
        chip_sums[s, target] = (
            chip_sums[s, target].astype(jnp.float32) + relay_landed[s].astype(jnp.float32)
        ).astype(jnp.bfloat16)

    def relay_sum(s):
        if not relayed:
            return

        @pl.when(chip == 1)
        def _():
            add_relayed(s, last)
            chip_copy(s, chips - 3).start()

        @pl.when(chip == last - 1)
        def _():
            add_relayed(s, 0)
            chip_copy(s, 1).start()

    products(0)
    products(1)
    chip_sum(0)

    def products_step(s, carry):
        products(s)
        chip_sum(s - 1)
        relay_sum(s - 2)
        return carry

    lax.fori_loop(2, sections, products_step, 0)
    chip_sum(sections - 1)
    relay_sum(sections - 2)
    relay_sum(sections - 1)

    def finish(s, carry):
        total_ref[...] = terms[s, core, chip].astype(jnp.float32) + sibling_terms[
            s, chip
        ].astype(jnp.float32)
        for d in range(chips - 1):

            def add(d=d):
                chip_copy(s, d).wait_recv()
                total_ref[...] += chip_landed[s, d].astype(jnp.float32)

            when_not(not_received(d), add)
        final_out[s] = total_ref[...].astype(jnp.bfloat16)

        @pl.when(s != me)
        def _():
            final_copy(s, me).start()

        @pl.when(s == me)
        def _():
            final_landed[s] = final_out[s]

        return carry

    lax.fori_loop(0, sections, finish, 0)

    def collect(s, carry):
        @pl.when(s != me)
        def _():
            final_copy(s, s).wait_recv()

        gradient_ref[s] = final_landed[s]
        return carry

    lax.fori_loop(0, sections, collect, 0)

    for d in range(sections - 1):
        rows_copy(peers[d], d, me).wait_send()
        gains_copy(peers[d], d, me).wait_send()

    def drain_rows(s, carry):
        for slot in range(chips):
            sibling_copy(s, slot, chip).wait_send()
        for d in range(chips - 1):
            when_not(not_sent(d), chip_copy(s, d).wait_send)
        if relayed:
            pl.when((chip == 1) | (chip == last - 1))(onward_high(s).wait_send)
            pl.when((chip == 0) | (chip == last))(from_low(s).wait_send)
        pair_copy(s).wait_send()

        @pl.when(s != me)
        def _():
            final_copy(s, me).wait_send()

        return carry

    rows_left(sections - 1)
    lax.fori_loop(0, sections, drain_rows, 0)

    def drain(step, carry):
        for h in range(HALVES):
            for copy in to_owners(step, h) + to_all(active, 0, step, h):
                copy.wait_send()
        return carry

    def drain_back(step, carry):
        for h in range(HALVES):
            for copy in to_owners(step, h) + to_all(grad_scaled, 0, step, h):
                copy.wait_send()
        return carry

    lax.fori_loop(0, sections, drain, 0)
    lax.fori_loop(sections, 2 * sections, drain_back, 0)
    for copy in sent:
        copy.wait_send()


def chain(tokens, cotangent, gains, owners, rows, shards, load_width, model_width):
    sections, _, part, width = rows.shape
    held = part * shards
    tok_rows = tokens.shape[0]
    block = tok_rows // sections
    chips = shards // 2
    vmem = pl.BlockSpec(memory_space=pltpu.VMEM)
    anywhere = pl.BlockSpec(memory_space=pl.ANY)
    owners_row = jnp.pad(owners.T, ((0, 8 - USERS_DEV), (0, 0)))
    owners = jnp.pad(owners, ((0, 0), (0, LANES - USERS_DEV)))
    steps = 2 * sections
    copies = (2 * steps * HALVES + 1, sections - 1)
    bf16, f32 = jnp.bfloat16, jnp.float32
    dma = pltpu.SemaphoreType.DMA
    return pl.pallas_call(
        functools.partial(chain_kernel, sections, model_width, load_width),
        out_shape=(
            jax.ShapeDtypeStruct(rows.shape, bf16),
            jax.ShapeDtypeStruct((8, LANES), f32),
        ),
        in_specs=[anywhere, anywhere, vmem, vmem, vmem, vmem],
        out_specs=(vmem, vmem),
        scratch_shapes=[
            pltpu.VMEM((sections, 2, held, width), bf16),
            pltpu.VMEM((sections, 1, held), f32),
            pltpu.VMEM((sections, tok_rows, held), bf16),
            pltpu.VMEM((sections, tok_rows, held), bf16),
            pltpu.VMEM((sections, tok_rows, held), bf16),
            pltpu.VMEM((sections, tok_rows, width), bf16),
            pltpu.VMEM((sections, tok_rows, width + LANES), bf16),
            pltpu.VMEM((sections, block, width), f32),
            pltpu.VMEM((sections, block, LANES), f32),
            pltpu.VMEM((tok_rows, width + LANES), f32),
            pltpu.VMEM((steps, tok_rows, width + LANES), bf16),
            pltpu.VMEM((steps, sections - 1, block, width + LANES), bf16),
            pltpu.VMEM((tok_rows, tok_rows), f32),
            pltpu.VMEM((sections, 8, LANES), f32),
            pltpu.VMEM((sections, 2, chips, 2, part, width), bf16),
            pltpu.VMEM((sections, chips, 2, part, width), bf16),
            pltpu.VMEM((sections, chips, 2, part, width), bf16),
            pltpu.VMEM((sections, chips - 1, 2, part, width), bf16),
            pltpu.VMEM((sections, 2, part, width), bf16),
            pltpu.VMEM((sections, 2, part, width), bf16),
            pltpu.VMEM((sections, 2, part, width), bf16),
            pltpu.VMEM((2, part, width), f32),
            dma(copies),
            dma(copies),
            dma((2, held // load_width)),
            dma((sections - 1,)),
            dma((sections,)),
            dma((sections - 1,)),
            dma((sections,)),
            dma((sections, chips - 1)),
            dma((sections, chips - 1)),
            dma((sections, chips)),
            dma((sections, chips)),
            dma((sections,)),
            dma((sections,)),
            dma((sections, chips - 1)),
            dma((sections, chips - 1)),
            dma((sections,)),
            dma((sections,)),
            dma((sections,)),
            dma((sections,)),
            dma((sections,)),
        ],
        compiler_params=pltpu.CompilerParams(
            collective_id=0, has_side_effects=True, vmem_limit_bytes=52 * 1024 * 1024
        ),
    )(tokens, cotangent, gains, owners, owners_row, rows)


def on_device(
    tokens, cotangent, lengths, seq_user, norm_gains, weights, first_moment, second_moment
):
    sections = lax.axis_size("section")
    quarter = lax.axis_index("section")
    shards = lax.axis_size("dp")
    tok_rows, model_width = tokens.shape
    own_rows, _, width = weights.shape[1:]
    part = own_rows // sections
    held = shards * part

    def own_features(values):
        split = values.reshape(tok_rows, shards, sections, part)
        return lax.dynamic_index_in_dim(split, quarter, 2, keepdims=False).reshape(tok_rows, held)

    low = weights[0].astype(jnp.bfloat16).reshape(sections, part, 2, width)
    low = low.transpose(0, 2, 1, 3)
    gains = norm_gains[0].reshape(shards, sections, part).transpose(1, 0, 2)
    gains = gains.reshape(sections, 1, held)

    positions = jnp.arange(tok_rows) % SEQLEN
    usable = positions < jnp.repeat(lengths, SEQLEN)
    local_user = seq_user - lax.axis_index("dp") * USERS_DEV
    token_user = jnp.repeat(local_user, SEQLEN)
    owners = ((token_user[:, None] == jnp.arange(USERS_DEV)[None, :]) & usable[:, None]).astype(
        jnp.float32
    )

    load_width = part
    if part % LANES != 0:
        tokens, cotangent, load_width = own_features(tokens), own_features(cotangent), held
    gradient, norms = chain(
        tokens, cotangent, gains, owners, low, shards, load_width, model_width
    )
    user_norm = norms[:USERS_DEV, 0]
    gradient = gradient.transpose(0, 2, 1, 3).reshape(own_rows, 2, width)
    gradient = with_layout_constraint(gradient, Layout((0, 1, 2))).astype(jnp.float32)
    moment_one = BETA_ONE * first_moment[0] + (1.0 - BETA_ONE) * gradient
    moment_two = BETA_TWO * second_moment[0] + (1.0 - BETA_TWO) * gradient * gradient
    direction = moment_one / FIRST_FIX / (jnp.sqrt(moment_two / SECOND_FIX) + ADAM_EPS)
    return (moment_one[None], moment_two[None], direction[None], user_norm / CLIP_BOUND)


def solution(mesh):
    return jax.shard_map(
        on_device,
        mesh=mesh,
        in_specs=(
            P("dp", None),
            P("dp", None),
            P("dp"),
            P("dp"),
            P("section", None),
            P("section", "dp", None, None),
            P("section", "dp", None, None),
            P("section", "dp", None, None),
        ),
        out_specs=(
            P("section", "dp", None, None),
            P("section", "dp", None, None),
            P("section", "dp", None, None),
            P("dp"),
        ),
        check_vma=False,
    )
```

```python
import functools

import jax
import jax.numpy as jnp
from jax import lax
from jax.experimental import pallas as pl
from jax.experimental.layout import Layout, with_layout_constraint
from jax.experimental.pallas import tpu as pltpu
from jax.sharding import PartitionSpec as P

SEQLEN = 64
USERS_DEV = 2


CLIP_BOUND = 70000.0
LOSS_SCALE = 1024.0
BETA_ONE = 0.9
BETA_TWO = 0.999
FIRST_FIX = 1.0 - 0.9**50
SECOND_FIX = 1.0 - 0.999**50
ADAM_EPS = 1e-08
NORM_EPS = 1e-05
LANES = 128
HALVES = 2


def dot_nt(left, right):
    return lax.dot_general(
        left, right, (((1,), (1,)), ((), ())), preferred_element_type=jnp.float32
    )


def dot_tn(left, right):
    return lax.dot_general(
        left, right, (((0,), (0,)), ((), ())), preferred_element_type=jnp.float32
    )


def split_lanes(column, rows):
    wide = jnp.broadcast_to(column, (rows, LANES))
    high = wide.astype(jnp.bfloat16).astype(jnp.float32)
    lane = lax.broadcasted_iota(jnp.int32, (rows, LANES), 1)
    return jnp.where(lane < LANES // 2, high, wide - high).astype(jnp.bfloat16)


def joined_lanes(block, start):
    high = block[:, start : start + 1].astype(jnp.float32)
    return high + block[:, start + LANES // 2 : start + LANES // 2 + 1].astype(jnp.float32)


def chain_kernel(
    sections,
    model_width,
    load_width,
    tokens_ref,
    cotangent_ref,
    own_gains_ref,
    owners_ref,
    owners_row_ref,
    rows_ref,
    gradient_ref,
    norm_ref,
    low,
    gains,
    hidden,
    scaled,
    grad_out,
    active,
    grad_scaled,
    inner,
    inverse,
    own_part,
    outgoing,
    landed,
    joint,
    squares,
    terms,
    sibling_terms,
    chip_sums,
    chip_landed,
    final_out,
    final_landed,
    relay_landed,
    total_ref,
    send_sem,
    recv_sem,
    load_sem,
    rows_send,
    rows_recv,
    gains_send,
    gains_recv,
    along_send,
    along_recv,
    sibling_send,
    sibling_recv,
    pair_send,
    pair_recv,
    chip_send,
    chip_recv,
    final_send,
    final_recv,
    onward_send,
    relay_send,
    relay_recv,
):
    me = lax.axis_index("section")
    place = lax.axis_index("dp")
    chips = lax.axis_size("dp") // 2
    chip, core = place // 2, lax.rem(place, 2)
    sibling = chip * 2 + 1 - core
    _, tok_rows, held = hidden.shape
    width = active.shape[2]
    part = rows_ref.shape[2]
    half = tok_rows // HALVES
    block = half // sections
    whole = [pl.ds(h * half, half) for h in range(HALVES)]
    mine = [pl.ds(h * block, block) for h in range(HALVES)]
    peers = [lax.rem(me + d, sections) for d in range(1, sections)]

    barrier = pltpu.get_barrier_semaphore()
    for peer in peers:
        pl.semaphore_signal(
            barrier, inc=1, device_id={"section": peer}, device_id_type=pl.DeviceIdType.MESH
        )
    ahead = [lax.rem(chip + d, chips) for d in range(1, chips)]
    behind = [lax.rem(chip + chips - d, chips) for d in range(1, chips)]
    for other in [sibling] + [a * 2 + core for a in ahead]:
        pl.semaphore_signal(
            barrier, inc=1, device_id={"dp": other}, device_id_type=pl.DeviceIdType.MESH
        )
    pl.semaphore_wait(barrier, sections - 1 + chips)

    def remote(source, target, sent, received, axis, index):
        return pltpu.make_async_remote_copy(
            src_ref=source,
            dst_ref=target,
            send_sem=sent,
            recv_sem=received,
            device_id={axis: index},
            device_id_type=pl.DeviceIdType.MESH,
        )

    def shard(s, at_chip, at_core):
        row = pl.multiple_of((at_chip * 2 + at_core) * part, part)
        return low.at[s, :, pl.ds(row, part)]

    pieces = held // load_width
    loads = []
    for which, (source, target) in enumerate(
        ((tokens_ref, hidden.at[0]), (cotangent_ref, grad_out.at[sections - 1]))
    ):
        for piece in range(pieces):
            first = (piece * sections + me) * load_width if pieces > 1 else 0
            loads.append(
                pltpu.make_async_copy(
                    source.at[:, pl.ds(pl.multiple_of(first, load_width), load_width)],
                    target.at[:, pl.ds(piece * load_width, load_width)],
                    load_sem.at[which, piece],
                )
            )

    def rows_copy(target, slot, source):
        return remote(
            rows_ref.at[target], shard(me, chip, core), rows_send.at[slot], rows_recv.at[source],
            "section", target,
        )

    def gains_copy(target, slot, source):
        return remote(
            own_gains_ref.at[target], gains.at[me], gains_send.at[slot], gains_recv.at[source],
            "section", target,
        )

    def along_copy(s, d):
        return remote(
            shard(s, chip, core), shard(s, chip, core), along_send.at[s, d], along_recv.at[s, d],
            "dp", ahead[d] * 2 + core,
        )

    def sibling_copy(s, slot, at_chip):
        return remote(
            shard(s, at_chip, core), shard(s, at_chip, core),
            sibling_send.at[s, slot], sibling_recv.at[s, slot], "dp", sibling,
        )

    for d in range(sections - 1):
        rows_copy(peers[d], d, me).start()
        gains_copy(peers[d], d, me).start()
    for load in loads:
        load.start()
    low[me, :, pl.ds(pl.multiple_of(place * part, part), part)] = rows_ref[me]
    gains[me] = own_gains_ref[me]

    last = chips - 1
    relayed = chips >= 4

    def when_not(excluded, run):
        if not excluded:
            run()
            return
        allowed = chip != excluded[0]
        for other in excluded[1:]:
            allowed = allowed & (chip != other)
        pl.when(allowed)(run)

    def not_sent(d):
        return [c for c, at in ((0, chips - 2), (last, 0)) if relayed and d == at]

    def held_back(d):
        return [c for c, at in ((1, chips - 3), (last - 1, 1)) if relayed and d == at]

    def not_received(d):
        return [c for c, at in ((last, chips - 2), (0, 0)) if relayed and d == at]

    def spread_rows(s):
        @pl.when(s != me)
        def _():
            rows_copy(peers[0], 0, s).wait_recv()
            gains_copy(peers[0], 0, s).wait_recv()

        sibling_copy(s, 0, chip).start()
        for d in range(chips - 1):
            when_not(not_sent(d), along_copy(s, d).start)

    def rows_left(s):
        for d in range(chips - 1):
            when_not(not_sent(d), along_copy(s, d).wait_send)

    def onward_high(s):
        return remote(
            shard(s, 0, core), shard(s, 0, core), onward_send.at[s],
            along_recv.at[s, chips - 2], "dp", last * 2 + core,
        )

    def onward_low(s):
        return remote(
            shard(s, last, core), shard(s, last, core), onward_send.at[s],
            along_recv.at[s, 0], "dp", core,
        )

    spread_rows(0)
    rows_left(0)
    spread_rows(1)

    def copies(make, slot):
        return [
            pltpu.make_async_remote_copy(
                src_ref=source,
                dst_ref=target,
                send_sem=send_sem.at[slot, d],
                recv_sem=recv_sem.at[slot, d],
                device_id={"section": peers[d]},
                device_id_type=pl.DeviceIdType.MESH,
            )
            for d in range(sections - 1)
            for source, target in [make(d)]
        ]

    def block_of(h, index):
        return pl.ds(pl.multiple_of(h * half + index * block, block), block)

    def to_owners(step, h):
        def make(d):
            return outgoing.at[step, block_of(h, peers[d])], landed.at[step, d, mine[h]]

        return copies(make, 2 * step * HALVES + h)

    def to_all(ref, s, step, h):
        def make(d):
            return ref.at[s, block_of(h, me)], ref.at[s, block_of(h, me)]

        return copies(make, (2 * step + 1) * HALVES + h)

    def start(sent):
        for copy in sent:
            copy.start()

    def arrived(sent):
        for copy in sent:
            copy.wait_recv()

    joint[...] = jnp.zeros_like(joint)
    for load in loads:
        load.wait()
    usable = owners_ref[:, :1]
    for user in range(1, USERS_DEV):
        usable = usable + owners_ref[:, user : user + 1]
    grad_out[sections - 1] = (grad_out[sections - 1].astype(jnp.float32) * usable).astype(
        jnp.bfloat16
    )

    def forward(s, carry):
        for d in [*range(1, chips - 2), 0, chips - 2] if relayed else range(chips - 1):
            along_copy(s, d).wait_recv()
            if relayed and d == chips - 3:
                pl.when(chip == last - 1)(onward_high(s).start)
            if relayed and d == 1:
                pl.when(chip == 1)(onward_low(s).start)
            sibling_copy(s, d + 1, behind[d]).start()
        for slot in range(chips):
            sibling_copy(s, slot, chip).wait_recv()
        for h in range(HALVES):

            @pl.when(s > 0)
            def _():
                arrived(to_all(active, s - 1, s - 1, h))
                branch = dot_nt(active[s - 1, whole[h]], low[s - 1, 1])
                hidden[s, whole[h]] = (
                    hidden[s - 1, whole[h]].astype(jnp.float32) + branch
                ).astype(jnp.bfloat16)

            widened = hidden[s, whole[h]].astype(jnp.float32)
            now = (widened * gains[s]).astype(jnp.bfloat16)
            scaled[s, whole[h]] = now
            product = jnp.dot(now, low[s, 0], preferred_element_type=jnp.float32)
            square = jnp.sum(widened * widened, axis=-1, keepdims=True)
            own_part[whole[h], :width] = product
            own_part[whole[h], width:] = jnp.broadcast_to(square, (half, LANES))
            outgoing[s, whole[h], :width] = product.astype(jnp.bfloat16)
            outgoing[s, whole[h], width:] = split_lanes(square, half)
            start(to_owners(s, h))

        @pl.when(s + 2 < sections)
        def _():
            rows_left(s + 1)
            spread_rows(s + 2)

        for h in range(HALVES):
            arrived(to_owners(s, h))
            total = own_part[block_of(h, me), :width]
            mean = own_part[block_of(h, me), width : width + 1]
            for d in range(sections - 1):
                piece = landed[s, d, mine[h]]
                total = total + piece[:, :width].astype(jnp.float32)
                mean = mean + joined_lanes(piece, width)
            scale = lax.rsqrt(mean / model_width + NORM_EPS)
            value = total * scale
            inner[s, mine[h]] = value
            inverse[s, mine[h]] = jnp.broadcast_to(scale, (block, LANES))
            active[s, block_of(h, me)] = (value / (1.0 + jnp.exp(-value))).astype(jnp.bfloat16)
            start(to_all(active, s, s, h))
        return carry

    lax.fori_loop(0, sections, forward, 0)
    for h in range(HALVES):
        arrived(to_all(active, sections - 1, sections - 1, h))

    def inner_gram(s):
        low_grad = grad_scaled[s, :, :width]
        joint[...] += dot_nt(scaled[s], scaled[s]) * dot_nt(low_grad, low_grad)

    def backward(back, carry):
        s = sections - 1 - back
        step = sections + back
        for h in range(HALVES):

            @pl.when(back > 0)
            def _():
                arrived(to_all(grad_scaled, s + 1, step - 1, h))
                block_in = grad_scaled[s + 1, whole[h]]
                grad_out[s, whole[h]] = (
                    grad_out[s + 1, whole[h]].astype(jnp.float32)
                    + gains[s + 1] * dot_nt(block_in[:, :width], low[s + 1, 0])
                    - hidden[s + 1, whole[h]].astype(jnp.float32) * joined_lanes(block_in, width)
                ).astype(jnp.bfloat16)

            product = jnp.dot(
                grad_out[s, whole[h]], low[s, 1], preferred_element_type=jnp.float32
            )
            own_part[whole[h], :width] = product
            outgoing[step, whole[h], :width] = product.astype(jnp.bfloat16)
            start(to_owners(step, h))

        joint[...] += dot_nt(active[s], active[s]) * dot_nt(grad_out[s], grad_out[s])
        for h in range(HALVES):
            arrived(to_owners(step, h))
            total = own_part[block_of(h, me), :width]
            for d in range(sections - 1):
                total = total + landed[step, d, mine[h], :width].astype(jnp.float32)
            value = inner[s, mine[h]]
            scale = inverse[s, mine[h]][:, :1]
            sigmoid_val = 1.0 / (1.0 + jnp.exp(-value))
            grad_inner = total * sigmoid_val * (1.0 + value * (1.0 - sigmoid_val))
            pull = jnp.sum(grad_inner * value, axis=-1, keepdims=True) * (
                scale * scale / model_width
            )
            grad_scaled[s, block_of(h, me), :width] = (grad_inner * scale).astype(jnp.bfloat16)
            grad_scaled[s, block_of(h, me), width:] = split_lanes(pull, block)
            start(to_all(grad_scaled, s, step, h))

        @pl.when(back > 0)
        def _():
            inner_gram(s + 1)

        return carry

    lax.fori_loop(0, sections, backward, 0)
    for h in range(HALVES):
        arrived(to_all(grad_scaled, 0, 2 * sections - 1, h))
    inner_gram(0)

    row_of = lax.broadcasted_iota(jnp.int32, (8, LANES), 0)
    sums = jnp.zeros((8, LANES), jnp.float32)
    for user in range(USERS_DEV):
        spread = joint[...] * owners_row_ref[user : user + 1, :]
        held_sum = jnp.sum(spread, axis=-1, keepdims=True) * owners_ref[:, user : user + 1]
        whole_sum = jnp.sum(held_sum, axis=0, keepdims=True)
        sums = jnp.where(row_of == user, whole_sum, sums)
    squares[me] = sums
    sent = copies(lambda d: (squares.at[me], squares.at[me]), 4 * sections * HALVES)
    start(sent)
    arrived(sent)
    total = squares[0]
    for s in range(1, sections):
        total = total + squares[s]
    user_norm = jnp.sqrt(total)
    norm_ref[...] = user_norm
    factors = LOSS_SCALE / jnp.maximum(user_norm, CLIP_BOUND)
    token_factor = owners_ref[:, :1] * factors[:1, :1]
    for user in range(1, USERS_DEV):
        token_factor = token_factor + owners_ref[:, user : user + 1] * factors[user : user + 1, :1]

    def pair_copy(s):
        return remote(
            terms.at[s, 1 - core], sibling_terms.at[s], pair_send.at[s], pair_recv.at[s],
            "dp", sibling,
        )

    def chip_copy(s, d):
        return remote(
            chip_sums.at[s, ahead[d]], chip_landed.at[s, d], chip_send.at[s, d],
            chip_recv.at[s, d], "dp", ahead[d] * 2 + core,
        )

    def final_copy(target, source):
        return remote(
            final_out.at[target], final_landed.at[me], final_send.at[target],
            final_recv.at[source], "section", target,
        )

    def products(s):
        weighted_inner = (grad_scaled[s, :, :width].astype(jnp.float32) * token_factor).astype(
            jnp.bfloat16
        )
        weighted_out = (grad_out[s].astype(jnp.float32) * token_factor).astype(jnp.bfloat16)
        down = dot_tn(scaled[s], weighted_inner).astype(jnp.bfloat16)
        up = dot_tn(weighted_out, active[s]).astype(jnp.bfloat16)
        for at_chip in range(chips):
            for at_core in range(2):
                row = (at_chip * 2 + at_core) * part
                terms[s, at_core, at_chip, 0] = down[row : row + part]
                terms[s, at_core, at_chip, 1] = up[row : row + part]
        pair_copy(s).start()

    def chip_sum(s):
        pair_copy(s).wait_recv()
        chip_sums[s] = (
            terms[s, core].astype(jnp.float32) + sibling_terms[s].astype(jnp.float32)
        ).astype(jnp.bfloat16)
        for d in range(chips - 1):
            when_not(not_sent(d) + held_back(d), chip_copy(s, d).start)
        if relayed:
            pl.when(chip == 0)(from_low(s).start)
            pl.when(chip == last)(from_high(s).start)

    def from_low(s):
        return remote(
            chip_sums.at[s, last], relay_landed.at[s], relay_send.at[s], relay_recv.at[s],
            "dp", 2 + core,
        )

    def from_high(s):
        return remote(
            chip_sums.at[s, 0], relay_landed.at[s], relay_send.at[s], relay_recv.at[s],
            "dp", (last - 1) * 2 + core,
        )

    def add_relayed(s, target):
        from_low(s).wait_recv()
        chip_sums[s, target] = (
            chip_sums[s, target].astype(jnp.float32) + relay_landed[s].astype(jnp.float32)
        ).astype(jnp.bfloat16)

    def relay_sum(s):
        if not relayed:
            return

        @pl.when(chip == 1)
        def _():
            add_relayed(s, last)
            chip_copy(s, chips - 3).start()

        @pl.when(chip == last - 1)
        def _():
            add_relayed(s, 0)
            chip_copy(s, 1).start()

    products(0)
    chip_sum(0)

    def products_step(s, carry):
        products(s)
        chip_sum(s)
        relay_sum(s - 1)
        return carry

    lax.fori_loop(1, sections, products_step, 0)
    relay_sum(sections - 1)

    def finish(s, carry):
        total_ref[...] = terms[s, core, chip].astype(jnp.float32) + sibling_terms[
            s, chip
        ].astype(jnp.float32)
        for d in range(chips - 1):

            def add(d=d):
                chip_copy(s, d).wait_recv()
                total_ref[...] += chip_landed[s, d].astype(jnp.float32)

            when_not(not_received(d), add)
        final_out[s] = total_ref[...].astype(jnp.bfloat16)

        @pl.when(s != me)
        def _():
            final_copy(s, me).start()

        @pl.when(s == me)
        def _():
            final_landed[s] = final_out[s]

        return carry

    lax.fori_loop(0, sections, finish, 0)

    def collect(s, carry):
        @pl.when(s != me)
        def _():
            final_copy(s, s).wait_recv()

        gradient_ref[s] = final_landed[s]
        return carry

    lax.fori_loop(0, sections, collect, 0)

    for d in range(sections - 1):
        rows_copy(peers[d], d, me).wait_send()
        gains_copy(peers[d], d, me).wait_send()

    def drain_rows(s, carry):
        for slot in range(chips):
            sibling_copy(s, slot, chip).wait_send()
        for d in range(chips - 1):
            when_not(not_sent(d), chip_copy(s, d).wait_send)
        if relayed:
            pl.when((chip == 1) | (chip == last - 1))(onward_high(s).wait_send)
            pl.when((chip == 0) | (chip == last))(from_low(s).wait_send)
        pair_copy(s).wait_send()

        @pl.when(s != me)
        def _():
            final_copy(s, me).wait_send()

        return carry

    rows_left(sections - 1)
    lax.fori_loop(0, sections, drain_rows, 0)

    def drain(step, carry):
        for h in range(HALVES):
            for copy in to_owners(step, h) + to_all(active, 0, step, h):
                copy.wait_send()
        return carry

    def drain_back(step, carry):
        for h in range(HALVES):
            for copy in to_owners(step, h) + to_all(grad_scaled, 0, step, h):
                copy.wait_send()
        return carry

    lax.fori_loop(0, sections, drain, 0)
    lax.fori_loop(sections, 2 * sections, drain_back, 0)
    for copy in sent:
        copy.wait_send()


def chain(tokens, cotangent, gains, owners, rows, shards, load_width, model_width):
    sections, _, part, width = rows.shape
    held = part * shards
    tok_rows = tokens.shape[0]
    block = tok_rows // sections
    chips = shards // 2
    vmem = pl.BlockSpec(memory_space=pltpu.VMEM)
    anywhere = pl.BlockSpec(memory_space=pl.ANY)
    owners_row = jnp.pad(owners.T, ((0, 8 - USERS_DEV), (0, 0)))
    owners = jnp.pad(owners, ((0, 0), (0, LANES - USERS_DEV)))
    steps = 2 * sections
    copies = (2 * steps * HALVES + 1, sections - 1)
    bf16, f32 = jnp.bfloat16, jnp.float32
    dma = pltpu.SemaphoreType.DMA
    return pl.pallas_call(
        functools.partial(chain_kernel, sections, model_width, load_width),
        out_shape=(
            jax.ShapeDtypeStruct(rows.shape, bf16),
            jax.ShapeDtypeStruct((8, LANES), f32),
        ),
        in_specs=[anywhere, anywhere, vmem, vmem, vmem, vmem],
        out_specs=(vmem, vmem),
        scratch_shapes=[
            pltpu.VMEM((sections, 2, held, width), bf16),
            pltpu.VMEM((sections, 1, held), f32),
            pltpu.VMEM((sections, tok_rows, held), bf16),
            pltpu.VMEM((sections, tok_rows, held), bf16),
            pltpu.VMEM((sections, tok_rows, held), bf16),
            pltpu.VMEM((sections, tok_rows, width), bf16),
            pltpu.VMEM((sections, tok_rows, width + LANES), bf16),
            pltpu.VMEM((sections, block, width), f32),
            pltpu.VMEM((sections, block, LANES), f32),
            pltpu.VMEM((tok_rows, width + LANES), f32),
            pltpu.VMEM((steps, tok_rows, width + LANES), bf16),
            pltpu.VMEM((steps, sections - 1, block, width + LANES), bf16),
            pltpu.VMEM((tok_rows, tok_rows), f32),
            pltpu.VMEM((sections, 8, LANES), f32),
            pltpu.VMEM((sections, 2, chips, 2, part, width), bf16),
            pltpu.VMEM((sections, chips, 2, part, width), bf16),
            pltpu.VMEM((sections, chips, 2, part, width), bf16),
            pltpu.VMEM((sections, chips - 1, 2, part, width), bf16),
            pltpu.VMEM((sections, 2, part, width), bf16),
            pltpu.VMEM((sections, 2, part, width), bf16),
            pltpu.VMEM((sections, 2, part, width), bf16),
            pltpu.VMEM((2, part, width), f32),
            dma(copies),
            dma(copies),
            dma((2, held // load_width)),
            dma((sections - 1,)),
            dma((sections,)),
            dma((sections - 1,)),
            dma((sections,)),
            dma((sections, chips - 1)),
            dma((sections, chips - 1)),
            dma((sections, chips)),
            dma((sections, chips)),
            dma((sections,)),
            dma((sections,)),
            dma((sections, chips - 1)),
            dma((sections, chips - 1)),
            dma((sections,)),
            dma((sections,)),
            dma((sections,)),
            dma((sections,)),
            dma((sections,)),
        ],
        compiler_params=pltpu.CompilerParams(
            collective_id=0, has_side_effects=True, vmem_limit_bytes=52 * 1024 * 1024
        ),
    )(tokens, cotangent, gains, owners, owners_row, rows)


def on_device(
    tokens, cotangent, lengths, seq_user, norm_gains, weights, first_moment, second_moment
):
    sections = lax.axis_size("section")
    quarter = lax.axis_index("section")
    shards = lax.axis_size("dp")
    tok_rows, model_width = tokens.shape
    own_rows, _, width = weights.shape[1:]
    part = own_rows // sections
    held = shards * part

    def own_features(values):
        split = values.reshape(tok_rows, shards, sections, part)
        return lax.dynamic_index_in_dim(split, quarter, 2, keepdims=False).reshape(tok_rows, held)

    low = weights[0].astype(jnp.bfloat16).reshape(sections, part, 2, width)
    low = low.transpose(0, 2, 1, 3)
    gains = norm_gains[0].reshape(shards, sections, part).transpose(1, 0, 2)
    gains = gains.reshape(sections, 1, held)

    positions = jnp.arange(tok_rows) % SEQLEN
    usable = positions < jnp.repeat(lengths, SEQLEN)
    local_user = seq_user - lax.axis_index("dp") * USERS_DEV
    token_user = jnp.repeat(local_user, SEQLEN)
    owners = ((token_user[:, None] == jnp.arange(USERS_DEV)[None, :]) & usable[:, None]).astype(
        jnp.float32
    )

    load_width = part
    if part % LANES != 0:
        tokens, cotangent, load_width = own_features(tokens), own_features(cotangent), held
    gradient, norms = chain(
        tokens, cotangent, gains, owners, low, shards, load_width, model_width
    )
    user_norm = norms[:USERS_DEV, 0]
    gradient = gradient.transpose(0, 2, 1, 3).reshape(own_rows, 2, width)
    gradient = with_layout_constraint(gradient, Layout((0, 1, 2))).astype(jnp.float32)
    moment_one = BETA_ONE * first_moment[0] + (1.0 - BETA_ONE) * gradient
    moment_two = BETA_TWO * second_moment[0] + (1.0 - BETA_TWO) * gradient * gradient
    direction = moment_one / FIRST_FIX / (jnp.sqrt(moment_two / SECOND_FIX) + ADAM_EPS)
    return (moment_one[None], moment_two[None], direction[None], user_norm / CLIP_BOUND)


def solution(mesh):
    return jax.shard_map(
        on_device,
        mesh=mesh,
        in_specs=(
            P("dp", None),
            P("dp", None),
            P("dp"),
            P("dp"),
            P("section", None),
            P("section", "dp", None, None),
            P("section", "dp", None, None),
            P("section", "dp", None, None),
        ),
        out_specs=(
            P("section", "dp", None, None),
            P("section", "dp", None, None),
            P("section", "dp", None, None),
            P("dp"),
        ),
        check_vma=False,
    )
```

```python
import functools

import jax
import jax.numpy as jnp
from jax import lax
from jax.experimental import pallas as pl
from jax.experimental.layout import Layout, with_layout_constraint
from jax.experimental.pallas import tpu as pltpu
from jax.sharding import PartitionSpec as P

SEQLEN = 64
USERS_DEV = 2


CLIP_BOUND = 70000.0
LOSS_SCALE = 1024.0
BETA_ONE = 0.9
BETA_TWO = 0.999
FIRST_FIX = 1.0 - 0.9**50
SECOND_FIX = 1.0 - 0.999**50
ADAM_EPS = 1e-08
NORM_EPS = 1e-05
LANES = 128
HALVES = 2


def dot_nt(left, right):
    return lax.dot_general(
        left, right, (((1,), (1,)), ((), ())), preferred_element_type=jnp.float32
    )


def dot_tn(left, right):
    return lax.dot_general(
        left, right, (((0,), (0,)), ((), ())), preferred_element_type=jnp.float32
    )


def split_lanes(column, rows):
    wide = jnp.broadcast_to(column, (rows, LANES))
    high = wide.astype(jnp.bfloat16).astype(jnp.float32)
    lane = lax.broadcasted_iota(jnp.int32, (rows, LANES), 1)
    return jnp.where(lane < LANES // 2, high, wide - high).astype(jnp.bfloat16)


def joined_lanes(block, start):
    high = block[:, start : start + 1].astype(jnp.float32)
    return high + block[:, start + LANES // 2 : start + LANES // 2 + 1].astype(jnp.float32)


def chain_kernel(
    sections,
    model_width,
    load_width,
    tokens_ref,
    cotangent_ref,
    own_gains_ref,
    owners_ref,
    owners_row_ref,
    rows_ref,
    gradient_ref,
    norm_ref,
    low,
    gains,
    hidden,
    scaled,
    grad_out,
    active,
    grad_scaled,
    inner,
    inverse,
    own_part,
    outgoing,
    landed,
    joint,
    squares,
    terms,
    sibling_terms,
    chip_sums,
    chip_landed,
    final_out,
    final_landed,
    relay_landed,
    total_ref,
    send_sem,
    recv_sem,
    load_sem,
    rows_send,
    rows_recv,
    gains_send,
    gains_recv,
    along_send,
    along_recv,
    sibling_send,
    sibling_recv,
    pair_send,
    pair_recv,
    chip_send,
    chip_recv,
    final_send,
    final_recv,
    onward_send,
    relay_send,
    relay_recv,
):
    me = lax.axis_index("section")
    place = lax.axis_index("dp")
    chips = lax.axis_size("dp") // 2
    chip, core = place // 2, lax.rem(place, 2)
    sibling = chip * 2 + 1 - core
    _, tok_rows, held = hidden.shape
    width = active.shape[2]
    part = rows_ref.shape[2]
    half = tok_rows // HALVES
    block = half // sections
    whole = [pl.ds(h * half, half) for h in range(HALVES)]
    mine = [pl.ds(h * block, block) for h in range(HALVES)]
    peers = [lax.rem(me + d, sections) for d in range(1, sections)]

    barrier = pltpu.get_barrier_semaphore()
    for peer in peers:
        pl.semaphore_signal(
            barrier, inc=1, device_id={"section": peer}, device_id_type=pl.DeviceIdType.MESH
        )
    ahead = [lax.rem(chip + d, chips) for d in range(1, chips)]
    behind = [lax.rem(chip + chips - d, chips) for d in range(1, chips)]
    for other in [sibling] + [a * 2 + core for a in ahead]:
        pl.semaphore_signal(
            barrier, inc=1, device_id={"dp": other}, device_id_type=pl.DeviceIdType.MESH
        )
    pl.semaphore_wait(barrier, sections - 1 + chips)

    def remote(source, target, sent, received, axis, index):
        return pltpu.make_async_remote_copy(
            src_ref=source,
            dst_ref=target,
            send_sem=sent,
            recv_sem=received,
            device_id={axis: index},
            device_id_type=pl.DeviceIdType.MESH,
        )

    def shard(s, at_chip, at_core):
        row = pl.multiple_of((at_chip * 2 + at_core) * part, part)
        return low.at[s, :, pl.ds(row, part)]

    pieces = held // load_width
    loads = []
    for which, (source, target) in enumerate(
        ((tokens_ref, hidden.at[0]), (cotangent_ref, grad_out.at[sections - 1]))
    ):
        for piece in range(pieces):
            first = (piece * sections + me) * load_width if pieces > 1 else 0
            loads.append(
                pltpu.make_async_copy(
                    source.at[:, pl.ds(pl.multiple_of(first, load_width), load_width)],
                    target.at[:, pl.ds(piece * load_width, load_width)],
                    load_sem.at[which, piece],
                )
            )

    def rows_copy(target, slot, source):
        return remote(
            rows_ref.at[target], shard(me, chip, core), rows_send.at[slot], rows_recv.at[source],
            "section", target,
        )

    def gains_copy(target, slot, source):
        return remote(
            own_gains_ref.at[target], gains.at[me], gains_send.at[slot], gains_recv.at[source],
            "section", target,
        )

    def along_copy(s, d):
        return remote(
            shard(s, chip, core), shard(s, chip, core), along_send.at[s, d], along_recv.at[s, d],
            "dp", ahead[d] * 2 + core,
        )

    def sibling_copy(s, slot, at_chip):
        return remote(
            shard(s, at_chip, core), shard(s, at_chip, core),
            sibling_send.at[s, slot], sibling_recv.at[s, slot], "dp", sibling,
        )

    for d in range(sections - 1):
        rows_copy(peers[d], d, me).start()
        gains_copy(peers[d], d, me).start()
    for load in loads:
        load.start()
    low[me, :, pl.ds(pl.multiple_of(place * part, part), part)] = rows_ref[me]
    gains[me] = own_gains_ref[me]

    last = chips - 1
    relayed = chips >= 4

    def when_not(excluded, run):
        if not excluded:
            run()
            return
        allowed = chip != excluded[0]
        for other in excluded[1:]:
            allowed = allowed & (chip != other)
        pl.when(allowed)(run)

    def not_sent(d):
        return [c for c, at in ((0, chips - 2), (last, 0)) if relayed and d == at]

    def held_back(d):
        return [c for c, at in ((1, chips - 3), (last - 1, 1)) if relayed and d == at]

    def not_received(d):
        return [c for c, at in ((last, chips - 2), (0, 0)) if relayed and d == at]

    def spread_rows(s):
        @pl.when(s != me)
        def _():
            rows_copy(peers[0], 0, s).wait_recv()
            gains_copy(peers[0], 0, s).wait_recv()

        sibling_copy(s, 0, chip).start()
        for d in range(chips - 1):
            when_not(not_sent(d), along_copy(s, d).start)

    def rows_left(s):
        for d in range(chips - 1):
            when_not(not_sent(d), along_copy(s, d).wait_send)

    def onward_high(s):
        return remote(
            shard(s, 0, core), shard(s, 0, core), onward_send.at[s],
            along_recv.at[s, chips - 2], "dp", last * 2 + core,
        )

    def onward_low(s):
        return remote(
            shard(s, last, core), shard(s, last, core), onward_send.at[s],
            along_recv.at[s, 0], "dp", core,
        )

    spread_rows(0)
    spread_rows(1)

    def copies(make, slot):
        return [
            pltpu.make_async_remote_copy(
                src_ref=source,
                dst_ref=target,
                send_sem=send_sem.at[slot, d],
                recv_sem=recv_sem.at[slot, d],
                device_id={"section": peers[d]},
                device_id_type=pl.DeviceIdType.MESH,
            )
            for d in range(sections - 1)
            for source, target in [make(d)]
        ]

    def block_of(h, index):
        return pl.ds(pl.multiple_of(h * half + index * block, block), block)

    def to_owners(step, h):
        def make(d):
            return outgoing.at[step, block_of(h, peers[d])], landed.at[step, d, mine[h]]

        return copies(make, 2 * step * HALVES + h)

    def to_all(ref, s, step, h):
        def make(d):
            return ref.at[s, block_of(h, me)], ref.at[s, block_of(h, me)]

        return copies(make, (2 * step + 1) * HALVES + h)

    def start(sent):
        for copy in sent:
            copy.start()

    def arrived(sent):
        for copy in sent:
            copy.wait_recv()

    joint[...] = jnp.zeros_like(joint)
    for load in loads:
        load.wait()
    usable = owners_ref[:, :1]
    for user in range(1, USERS_DEV):
        usable = usable + owners_ref[:, user : user + 1]
    grad_out[sections - 1] = (grad_out[sections - 1].astype(jnp.float32) * usable).astype(
        jnp.bfloat16
    )

    def forward(s, carry):
        for d in [*range(1, chips - 2), 0, chips - 2] if relayed else range(chips - 1):
            along_copy(s, d).wait_recv()
            if relayed and d == chips - 3:
                pl.when(chip == last - 1)(onward_high(s).start)
            if relayed and d == 1:
                pl.when(chip == 1)(onward_low(s).start)
            sibling_copy(s, d + 1, behind[d]).start()
        for slot in range(chips):
            sibling_copy(s, slot, chip).wait_recv()
        for h in range(HALVES):

            @pl.when(s > 0)
            def _():
                arrived(to_all(active, s - 1, s - 1, h))
                branch = dot_nt(active[s - 1, whole[h]], low[s - 1, 1])
                hidden[s, whole[h]] = (
                    hidden[s - 1, whole[h]].astype(jnp.float32) + branch
                ).astype(jnp.bfloat16)

            widened = hidden[s, whole[h]].astype(jnp.float32)
            now = (widened * gains[s]).astype(jnp.bfloat16)
            scaled[s, whole[h]] = now
            product = jnp.dot(now, low[s, 0], preferred_element_type=jnp.float32)
            square = jnp.sum(widened * widened, axis=-1, keepdims=True)
            own_part[whole[h], :width] = product
            own_part[whole[h], width:] = jnp.broadcast_to(square, (half, LANES))
            outgoing[s, whole[h], :width] = product.astype(jnp.bfloat16)
            outgoing[s, whole[h], width:] = split_lanes(square, half)
            start(to_owners(s, h))

        @pl.when(s + 2 < sections)
        def _():
            rows_left(s)
            spread_rows(s + 2)

        for h in range(HALVES):
            arrived(to_owners(s, h))
            total = own_part[block_of(h, me), :width]
            mean = own_part[block_of(h, me), width : width + 1]
            for d in range(sections - 1):
                piece = landed[s, d, mine[h]]
                total = total + piece[:, :width].astype(jnp.float32)
                mean = mean + joined_lanes(piece, width)
            scale = lax.rsqrt(mean / model_width + NORM_EPS)
            value = total * scale
            inner[s, mine[h]] = value
            inverse[s, mine[h]] = jnp.broadcast_to(scale, (block, LANES))
            active[s, block_of(h, me)] = (value / (1.0 + jnp.exp(-value))).astype(jnp.bfloat16)
            start(to_all(active, s, s, h))
        return carry

    lax.fori_loop(0, sections, forward, 0)
    for h in range(HALVES):
        arrived(to_all(active, sections - 1, sections - 1, h))

    def inner_gram(s):
        low_grad = grad_scaled[s, :, :width]
        joint[...] += dot_nt(scaled[s], scaled[s]) * dot_nt(low_grad, low_grad)

    def backward(back, carry):
        s = sections - 1 - back
        step = sections + back
        for h in range(HALVES):

            @pl.when(back > 0)
            def _():
                arrived(to_all(grad_scaled, s + 1, step - 1, h))
                block_in = grad_scaled[s + 1, whole[h]]
                grad_out[s, whole[h]] = (
                    grad_out[s + 1, whole[h]].astype(jnp.float32)
                    + gains[s + 1] * dot_nt(block_in[:, :width], low[s + 1, 0])
                    - hidden[s + 1, whole[h]].astype(jnp.float32) * joined_lanes(block_in, width)
                ).astype(jnp.bfloat16)

            product = jnp.dot(
                grad_out[s, whole[h]], low[s, 1], preferred_element_type=jnp.float32
            )
            own_part[whole[h], :width] = product
            outgoing[step, whole[h], :width] = product.astype(jnp.bfloat16)
            start(to_owners(step, h))

        joint[...] += dot_nt(active[s], active[s]) * dot_nt(grad_out[s], grad_out[s])
        for h in range(HALVES):
            arrived(to_owners(step, h))
            total = own_part[block_of(h, me), :width]
            for d in range(sections - 1):
                total = total + landed[step, d, mine[h], :width].astype(jnp.float32)
            value = inner[s, mine[h]]
            scale = inverse[s, mine[h]][:, :1]
            sigmoid_val = 1.0 / (1.0 + jnp.exp(-value))
            grad_inner = total * sigmoid_val * (1.0 + value * (1.0 - sigmoid_val))
            pull = jnp.sum(grad_inner * value, axis=-1, keepdims=True) * (
                scale * scale / model_width
            )
            grad_scaled[s, block_of(h, me), :width] = (grad_inner * scale).astype(jnp.bfloat16)
            grad_scaled[s, block_of(h, me), width:] = split_lanes(pull, block)
            start(to_all(grad_scaled, s, step, h))

        @pl.when(back > 0)
        def _():
            inner_gram(s + 1)

        return carry

    lax.fori_loop(0, sections, backward, 0)
    for h in range(HALVES):
        arrived(to_all(grad_scaled, 0, 2 * sections - 1, h))
    inner_gram(0)

    row_of = lax.broadcasted_iota(jnp.int32, (8, LANES), 0)
    sums = jnp.zeros((8, LANES), jnp.float32)
    for user in range(USERS_DEV):
        spread = joint[...] * owners_row_ref[user : user + 1, :]
        held_sum = jnp.sum(spread, axis=-1, keepdims=True) * owners_ref[:, user : user + 1]
        whole_sum = jnp.sum(held_sum, axis=0, keepdims=True)
        sums = jnp.where(row_of == user, whole_sum, sums)
    squares[me] = sums
    sent = copies(lambda d: (squares.at[me], squares.at[me]), 4 * sections * HALVES)
    start(sent)
    arrived(sent)
    total = squares[0]
    for s in range(1, sections):
        total = total + squares[s]
    user_norm = jnp.sqrt(total)
    norm_ref[...] = user_norm
    factors = LOSS_SCALE / jnp.maximum(user_norm, CLIP_BOUND)
    token_factor = owners_ref[:, :1] * factors[:1, :1]
    for user in range(1, USERS_DEV):
        token_factor = token_factor + owners_ref[:, user : user + 1] * factors[user : user + 1, :1]

    def pair_copy(s):
        return remote(
            terms.at[s, 1 - core], sibling_terms.at[s], pair_send.at[s], pair_recv.at[s],
            "dp", sibling,
        )

    def chip_copy(s, d):
        return remote(
            chip_sums.at[s, ahead[d]], chip_landed.at[s, d], chip_send.at[s, d],
            chip_recv.at[s, d], "dp", ahead[d] * 2 + core,
        )

    def final_copy(target, source):
        return remote(
            final_out.at[target], final_landed.at[me], final_send.at[target],
            final_recv.at[source], "section", target,
        )

    def products(s):
        weighted_inner = (grad_scaled[s, :, :width].astype(jnp.float32) * token_factor).astype(
            jnp.bfloat16
        )
        weighted_out = (grad_out[s].astype(jnp.float32) * token_factor).astype(jnp.bfloat16)
        down = dot_tn(scaled[s], weighted_inner).astype(jnp.bfloat16)
        up = dot_tn(weighted_out, active[s]).astype(jnp.bfloat16)
        for at_chip in range(chips):
            for at_core in range(2):
                row = (at_chip * 2 + at_core) * part
                terms[s, at_core, at_chip, 0] = down[row : row + part]
                terms[s, at_core, at_chip, 1] = up[row : row + part]
        pair_copy(s).start()

    def chip_sum(s):
        pair_copy(s).wait_recv()
        chip_sums[s] = (
            terms[s, core].astype(jnp.float32) + sibling_terms[s].astype(jnp.float32)
        ).astype(jnp.bfloat16)
        for d in range(chips - 1):
            when_not(not_sent(d) + held_back(d), chip_copy(s, d).start)
        if relayed:
            pl.when(chip == 0)(from_low(s).start)
            pl.when(chip == last)(from_high(s).start)

    def from_low(s):
        return remote(
            chip_sums.at[s, last], relay_landed.at[s], relay_send.at[s], relay_recv.at[s],
            "dp", 2 + core,
        )

    def from_high(s):
        return remote(
            chip_sums.at[s, 0], relay_landed.at[s], relay_send.at[s], relay_recv.at[s],
            "dp", (last - 1) * 2 + core,
        )

    def add_relayed(s, target):
        from_low(s).wait_recv()
        chip_sums[s, target] = (
            chip_sums[s, target].astype(jnp.float32) + relay_landed[s].astype(jnp.float32)
        ).astype(jnp.bfloat16)

    def relay_sum(s):
        if not relayed:
            return

        @pl.when(chip == 1)
        def _():
            add_relayed(s, last)
            chip_copy(s, chips - 3).start()

        @pl.when(chip == last - 1)
        def _():
            add_relayed(s, 0)
            chip_copy(s, 1).start()

    products(0)
    chip_sum(0)

    def products_step(s, carry):
        products(s)
        chip_sum(s)
        relay_sum(s - 1)
        return carry

    lax.fori_loop(1, sections, products_step, 0)
    relay_sum(sections - 1)

    def finish(s, carry):
        total_ref[...] = terms[s, core, chip].astype(jnp.float32) + sibling_terms[
            s, chip
        ].astype(jnp.float32)
        for d in range(chips - 1):

            def add(d=d):
                chip_copy(s, d).wait_recv()
                total_ref[...] += chip_landed[s, d].astype(jnp.float32)

            when_not(not_received(d), add)
        final_out[s] = total_ref[...].astype(jnp.bfloat16)

        @pl.when(s != me)
        def _():
            final_copy(s, me).start()

        @pl.when(s == me)
        def _():
            final_landed[s] = final_out[s]

        return carry

    lax.fori_loop(0, sections, finish, 0)

    def collect(s, carry):
        @pl.when(s != me)
        def _():
            final_copy(s, s).wait_recv()

        gradient_ref[s] = final_landed[s]
        return carry

    lax.fori_loop(0, sections, collect, 0)

    for d in range(sections - 1):
        rows_copy(peers[d], d, me).wait_send()
        gains_copy(peers[d], d, me).wait_send()

    def drain_rows(s, carry):
        for slot in range(chips):
            sibling_copy(s, slot, chip).wait_send()
        for d in range(chips - 1):
            when_not(not_sent(d), chip_copy(s, d).wait_send)
        if relayed:
            pl.when((chip == 1) | (chip == last - 1))(onward_high(s).wait_send)
            pl.when((chip == 0) | (chip == last))(from_low(s).wait_send)
        pair_copy(s).wait_send()

        @pl.when(s != me)
        def _():
            final_copy(s, me).wait_send()

        return carry

    rows_left(sections - 2)
    rows_left(sections - 1)
    lax.fori_loop(0, sections, drain_rows, 0)

    def drain(step, carry):
        for h in range(HALVES):
            for copy in to_owners(step, h) + to_all(active, 0, step, h):
                copy.wait_send()
        return carry

    def drain_back(step, carry):
        for h in range(HALVES):
            for copy in to_owners(step, h) + to_all(grad_scaled, 0, step, h):
                copy.wait_send()
        return carry

    lax.fori_loop(0, sections, drain, 0)
    lax.fori_loop(sections, 2 * sections, drain_back, 0)
    for copy in sent:
        copy.wait_send()


def chain(tokens, cotangent, gains, owners, rows, shards, load_width, model_width):
    sections, _, part, width = rows.shape
    held = part * shards
    tok_rows = tokens.shape[0]
    block = tok_rows // sections
    chips = shards // 2
    vmem = pl.BlockSpec(memory_space=pltpu.VMEM)
    anywhere = pl.BlockSpec(memory_space=pl.ANY)
    owners_row = jnp.pad(owners.T, ((0, 8 - USERS_DEV), (0, 0)))
    owners = jnp.pad(owners, ((0, 0), (0, LANES - USERS_DEV)))
    steps = 2 * sections
    copies = (2 * steps * HALVES + 1, sections - 1)
    bf16, f32 = jnp.bfloat16, jnp.float32
    dma = pltpu.SemaphoreType.DMA
    return pl.pallas_call(
        functools.partial(chain_kernel, sections, model_width, load_width),
        out_shape=(
            jax.ShapeDtypeStruct(rows.shape, bf16),
            jax.ShapeDtypeStruct((8, LANES), f32),
        ),
        in_specs=[anywhere, anywhere, vmem, vmem, vmem, vmem],
        out_specs=(vmem, vmem),
        scratch_shapes=[
            pltpu.VMEM((sections, 2, held, width), bf16),
            pltpu.VMEM((sections, 1, held), f32),
            pltpu.VMEM((sections, tok_rows, held), bf16),
            pltpu.VMEM((sections, tok_rows, held), bf16),
            pltpu.VMEM((sections, tok_rows, held), bf16),
            pltpu.VMEM((sections, tok_rows, width), bf16),
            pltpu.VMEM((sections, tok_rows, width + LANES), bf16),
            pltpu.VMEM((sections, block, width), f32),
            pltpu.VMEM((sections, block, LANES), f32),
            pltpu.VMEM((tok_rows, width + LANES), f32),
            pltpu.VMEM((steps, tok_rows, width + LANES), bf16),
            pltpu.VMEM((steps, sections - 1, block, width + LANES), bf16),
            pltpu.VMEM((tok_rows, tok_rows), f32),
            pltpu.VMEM((sections, 8, LANES), f32),
            pltpu.VMEM((sections, 2, chips, 2, part, width), bf16),
            pltpu.VMEM((sections, chips, 2, part, width), bf16),
            pltpu.VMEM((sections, chips, 2, part, width), bf16),
            pltpu.VMEM((sections, chips - 1, 2, part, width), bf16),
            pltpu.VMEM((sections, 2, part, width), bf16),
            pltpu.VMEM((sections, 2, part, width), bf16),
            pltpu.VMEM((sections, 2, part, width), bf16),
            pltpu.VMEM((2, part, width), f32),
            dma(copies),
            dma(copies),
            dma((2, held // load_width)),
            dma((sections - 1,)),
            dma((sections,)),
            dma((sections - 1,)),
            dma((sections,)),
            dma((sections, chips - 1)),
            dma((sections, chips - 1)),
            dma((sections, chips)),
            dma((sections, chips)),
            dma((sections,)),
            dma((sections,)),
            dma((sections, chips - 1)),
            dma((sections, chips - 1)),
            dma((sections,)),
            dma((sections,)),
            dma((sections,)),
            dma((sections,)),
            dma((sections,)),
        ],
        compiler_params=pltpu.CompilerParams(
            collective_id=0, has_side_effects=True, vmem_limit_bytes=52 * 1024 * 1024
        ),
    )(tokens, cotangent, gains, owners, owners_row, rows)


def on_device(
    tokens, cotangent, lengths, seq_user, norm_gains, weights, first_moment, second_moment
):
    sections = lax.axis_size("section")
    quarter = lax.axis_index("section")
    shards = lax.axis_size("dp")
    tok_rows, model_width = tokens.shape
    own_rows, _, width = weights.shape[1:]
    part = own_rows // sections
    held = shards * part

    def own_features(values):
        split = values.reshape(tok_rows, shards, sections, part)
        return lax.dynamic_index_in_dim(split, quarter, 2, keepdims=False).reshape(tok_rows, held)

    low = weights[0].astype(jnp.bfloat16).reshape(sections, part, 2, width)
    low = low.transpose(0, 2, 1, 3)
    gains = norm_gains[0].reshape(shards, sections, part).transpose(1, 0, 2)
    gains = gains.reshape(sections, 1, held)

    positions = jnp.arange(tok_rows) % SEQLEN
    usable = positions < jnp.repeat(lengths, SEQLEN)
    local_user = seq_user - lax.axis_index("dp") * USERS_DEV
    token_user = jnp.repeat(local_user, SEQLEN)
    owners = ((token_user[:, None] == jnp.arange(USERS_DEV)[None, :]) & usable[:, None]).astype(
        jnp.float32
    )

    load_width = part
    if part % LANES != 0:
        tokens, cotangent, load_width = own_features(tokens), own_features(cotangent), held
    gradient, norms = chain(
        tokens, cotangent, gains, owners, low, shards, load_width, model_width
    )
    user_norm = norms[:USERS_DEV, 0]
    gradient = gradient.transpose(0, 2, 1, 3).reshape(own_rows, 2, width)
    gradient = with_layout_constraint(gradient, Layout((0, 1, 2))).astype(jnp.float32)
    moment_one = BETA_ONE * first_moment[0] + (1.0 - BETA_ONE) * gradient
    moment_two = BETA_TWO * second_moment[0] + (1.0 - BETA_TWO) * gradient * gradient
    direction = moment_one / FIRST_FIX / (jnp.sqrt(moment_two / SECOND_FIX) + ADAM_EPS)
    return (moment_one[None], moment_two[None], direction[None], user_norm / CLIP_BOUND)


def solution(mesh):
    return jax.shard_map(
        on_device,
        mesh=mesh,
        in_specs=(
            P("dp", None),
            P("dp", None),
            P("dp"),
            P("dp"),
            P("section", None),
            P("section", "dp", None, None),
            P("section", "dp", None, None),
            P("section", "dp", None, None),
        ),
        out_specs=(
            P("section", "dp", None, None),
            P("section", "dp", None, None),
            P("section", "dp", None, None),
            P("dp"),
        ),
        check_vma=False,
    )
```
